256 devices in a mesh: group: 8 (over y, z_lo), dev: 32 (over z_hi, x, core).
Axes of the slice: x: 4, y: 4, z: 8 (z_hi: 4, z_lo: 2; z = z_hi * 2 + z_lo), core: 2. Of those that a mesh axis runs over, the one named last changes fastest.
Arguments:
- tokens: bfloat16 [4096, 2560], P(('group', 'dev')), may hold values from -6 to 6
- grad_out: bfloat16 [4096, 2560], P(('group', 'dev')), may hold values from -6 to 6
- routes: int32 [4096, 6], P(('group', 'dev')), may hold values from 0 to 23, all different within a row; in each aligned block of 16 rows (0 to 15, 16 to 31, ...) at most 6 rows name the same one
- gates: bfloat16 [4096, 6], P(('group', 'dev')), may hold values from 0.049804688 to 0.5
- pull_list: int32 [8, 8], replicated, may hold values from 0 to 127, as said below
- counts: int32 [8], replicated, may hold values from 1 to 512, 2304 in all
- w_gate: bfloat16 [256, 2560, 384], P(('group', 'dev')), may hold values from -0.125 to 0.125
- w_up: bfloat16 [256, 2560, 384], P(('group', 'dev')), may hold values from -0.125 to 0.125
- w_down: bfloat16 [256, 384, 2560], P(('group', 'dev')), may hold values from -0.21875 to 0.21875
Outputs:
- mixed: bfloat16 [4096, 2560], P(('group', 'dev'))
- token_grad: bfloat16 [4096, 2560], P(('group', 'dev'))
- grad_gate: bfloat16 [256, 2560, 384], P(('group', 'dev'))
- grad_up: bfloat16 [256, 2560, 384], P(('group', 'dev'))
- grad_down: bfloat16 [256, 384, 2560], P(('group', 'dev'))
The draws below stay inside these ranges and needn't reach their ends.
Inputs may be any that keep to these rules, and one draw needn't show every extreme that they name: `routes`: the rows of one device name each slot at most 6 times, a bound that some block reaches. `pull_list`: row g holds 8 distinct experts of group (g - 1) mod 8; expert e belongs to group e // 16. `counts`: some group has all its rows live.
All inputs are finite; a program needn't handle non-finite values.
Results may differ from the reference program's by a relative error of at most 0.01.
Values may be sent and summed in bfloat16 or wider, within the bound.
A program may use at most 128 MiB of HBM per device.

```python
import math
import jax
import jax.numpy as jnp
import numpy as np
from jax import lax

D = 2560
HID = 768
SLICES = 2
CHOSEN_EXPERTS = 6
DEVICE_TOKENS = 16
H_DEV = 384
EXP_GROUP = 16
PULL = 8
SLOT_OPTIONS = 24
EXPERTS = 128
SLOT_CEILING = 6
TOK_GROUP = 512
TOKEN_ROWS_ALL = 4096
N_GROUP = 8
N_DEV = 32


def draw_pull_list(key, part):
    key = jax.random.fold_in(key, 17)
    group_keys = jax.random.split(key, N_GROUP)

    def choose_local(one_key):
        return jax.random.permutation(one_key, EXP_GROUP)[:PULL]
    chosen = jax.vmap(choose_local)(group_keys)
    owners = jnp.mod(jnp.arange(N_GROUP) - 1, N_GROUP)
    return (owners[:, None] * EXP_GROUP + chosen).astype(jnp.int32)


def block_levels(rng, dims, cuts, smallest, largest):
    factor_of = 1.0
    for position, blocks in cuts:
        steps = jax.random.uniform(jax.random.fold_in(jax.random.fold_in(rng, 6), position), (blocks,), jnp.float32, smallest / len(cuts), largest / len(cuts))
        factor_of = factor_of * jnp.repeat(jnp.exp(steps), dims[position] // blocks).reshape((-1,) + (1,) * (len(dims) - 1 - position))
    return factor_of


def split_up(count, total, bound, slope):
    weights = [(1 << 20) // math.isqrt(standing ** slope) + 1 for standing in range(2, count + 1)]
    spare, given = total - bound - (count - 1), [1] * (count - 1)
    while spare > 0:
        free = [i for i in range(count - 1) if given[i] < bound]
        mass, budget = sum([weights[i] for i in free]), spare
        for i in free:
            addition = min(bound - given[i], max(1, budget * weights[i] // mass), spare)
            given[i] = given[i] + addition
            spare = spare - addition
    return np.array([bound] + given)


def ragged(stream_key, count, total, bound, slope):
    if count == 2:
        one = jax.random.randint(stream_key, (), max(1, total - bound), min(bound, total - 1) + 1)
        return jnp.stack([one, total - one])
    sizes = jnp.asarray(split_up(count, total, bound, slope), jnp.int32)
    twos = (count - 1) // 2
    donor, sink = sizes[1:1 + 2 * twos:2], sizes[2:2 + 2 * twos:2]
    slack = jnp.minimum(donor - 1, bound - sink)
    moved = jax.random.randint(jax.random.fold_in(stream_key, 1), (twos,), 0, 1 << 20) % (slack + 1)
    sizes = sizes.at[1:1 + 2 * twos:2].set(donor - moved).at[2:2 + 2 * twos:2].set(sink + moved)
    return sizes[jax.random.permutation(jax.random.fold_in(stream_key, 2), count)]


def shared_out(stream_key, own, number, rows, number_of, top, most, slope):
    order = jax.random.permutation(stream_key, number_of)
    heavy_load, common = load_shares(number_of, rows * top, most, slope, True), load_shares(number_of, rows * top, most, slope, False)
    places = jnp.arange(number_of)

    def named(tallies, offset_by):
        used = int((tallies > 0).sum())
        fixed = max(1, used // 4)
        shifted = fixed + (places - fixed + offset_by * (used - fixed)) % max(1, number_of - fixed)
        return jnp.zeros((number_of,), jnp.int32).at[order[jnp.where(places < fixed, places, shifted)]].set(jnp.asarray(tallies, jnp.int32))

    tallies = jnp.where(number % 4 == 0, named(heavy_load, number // 4), named(common, number - number // 4 - 1))
    mixed = jax.random.permutation(jax.random.fold_in(own, 3), number_of)
    donor, sink = mixed[0:number_of // 2 * 2:2], mixed[1:number_of // 2 * 2:2]
    margin = jnp.minimum(tallies[donor] - 1, most - tallies[sink]) // 2
    margin = jnp.where((donor == order[0]) | (sink == order[0]) | (tallies[sink] == 0), 0, jnp.maximum(margin, 0))
    shifted = jax.random.randint(jax.random.fold_in(own, 4), (number_of // 2,), 0, 1 << 20) % (margin + 1)
    tallies = tallies.at[donor].add(-shifted).at[sink].add(shifted)
    labels = jnp.searchsorted(jnp.cumsum(tallies), jnp.arange(rows * top), side="right").astype(jnp.int32)
    listing = labels.reshape(top, rows).T
    listing = listing[jax.random.permutation(jax.random.fold_in(own, 1), rows)]
    offset_by = jax.random.randint(jax.random.fold_in(own, 2), (rows, 1), 0, top)
    return jnp.take_along_axis(listing, (jnp.arange(top)[None, :] + offset_by) % top, axis=1)


def load_shares(count, total, reach, skew, full):
    portions = [(1 << 20) // math.isqrt(standing ** skew) + 1 for standing in range(1, count + 1)]
    largest = reach if full else min(reach, max(-(-total // count), total * portions[0] // sum(portions)))
    least = 1 if total - largest >= count - 1 else 0
    given, spare = [largest] + [least] * (count - 1), total - largest - least * (count - 1)
    while spare > 0:
        movable = [i for i in range(1, count) if given[i] < largest] or [i for i in range(1, count) if given[i] < reach]
        pool, budget = sum([portions[i] for i in movable]), spare
        for i in movable:
            extra = min(reach - given[i], max(1, budget * portions[i] // pool), spare)
            given[i] = given[i] + extra
            spare = spare - extra
    return np.array(given)


def noise(stream_key, extent, spread, most, cuts=(), kind=jnp.bfloat16):
    drawn = jax.random.normal(stream_key, extent, jnp.float32) * spread
    if len(cuts) > 0:
        drawn = block_levels(stream_key, extent, cuts, -0.22, 0.18) * drawn
    return jnp.clip(drawn, min=-most, max=most).astype(kind)


def setup_inputs(seed: int = 0) -> dict:
    seeds = jax.random.split(jax.random.key(seed), 10)
    tokens = noise(seeds[0], (TOKEN_ROWS_ALL, D), 1.0, 6.0, ((0, 256),))
    grad_out = noise(seeds[1], (TOKEN_ROWS_ALL, D), 1.0, 6.0, ((0, 256),))
    routes_keys = jax.random.split(jax.random.fold_in(seeds[2], 1), TOKEN_ROWS_ALL // DEVICE_TOKENS)
    routes_turns = jax.random.permutation(jax.random.fold_in(seeds[2], 3), TOKEN_ROWS_ALL // DEVICE_TOKENS)
    routes = jax.vmap(lambda own, number: shared_out(jax.random.fold_in(seeds[2], 2), own, number, DEVICE_TOKENS, SLOT_OPTIONS, CHOSEN_EXPERTS, SLOT_CEILING, 2))(routes_keys, routes_turns).reshape((TOKEN_ROWS_ALL, CHOSEN_EXPERTS))
    gates = jnp.clip(jnp.exp(math.log(0.5) - 2.306499 * jax.random.uniform(seeds[3], (TOKEN_ROWS_ALL, CHOSEN_EXPERTS), jnp.float32) ** block_levels(seeds[3], (TOKEN_ROWS_ALL, CHOSEN_EXPERTS), ((0, 256),), -0.2, 0.2)), 0.049804688, 0.5).astype(jnp.bfloat16)
    pull_list = draw_pull_list(jax.random.fold_in(seeds[9], 71), 0)
    counts = ragged(seeds[5], N_GROUP, (N_GROUP + 1) * TOK_GROUP // 2, TOK_GROUP, 2).astype(jnp.int32)
    w_gate = noise(seeds[6], (EXPERTS * SLICES, D, H_DEV), D ** -0.5, 0.125, ((0, 256),))
    w_up = noise(seeds[7], (EXPERTS * SLICES, D, H_DEV), D ** -0.5, 0.125, ((0, 256),))
    w_down = noise(seeds[8], (EXPERTS * SLICES, H_DEV, D), HID ** -0.5, 0.21875, ((0, 256),))
    return dict(tokens=tokens, grad_out=grad_out, routes=routes, gates=gates, pull_list=pull_list, counts=counts, w_gate=w_gate, w_up=w_up, w_down=w_down)


def expert_pass(rows_x, rows_dy, rows_gate, weight_gate, weight_up, weight_down):
    pre_gate = jnp.dot(rows_x, weight_gate, preferred_element_type=jnp.float32)
    pre_up = jnp.dot(rows_x, weight_up, preferred_element_type=jnp.float32)
    sigmoid_gate = jax.nn.sigmoid(pre_gate)
    activated = pre_gate * sigmoid_gate
    gate_scale = rows_gate.astype(jnp.float32)[:, None]
    gated_hidden = (gate_scale * activated * pre_up).astype(jnp.bfloat16)
    partial_out = jnp.dot(gated_hidden, weight_down, preferred_element_type=jnp.float32).astype(jnp.bfloat16)
    back_hidden = jnp.dot(rows_dy, weight_down.T, preferred_element_type=jnp.float32) * gate_scale
    grad_pre_gate = (back_hidden * pre_up * sigmoid_gate * (1.0 + pre_gate * (1.0 - sigmoid_gate))).astype(jnp.bfloat16)
    grad_pre_up = (back_hidden * activated).astype(jnp.bfloat16)
    partial_dx = (jnp.dot(grad_pre_gate, weight_gate.T, preferred_element_type=jnp.float32)
                  + jnp.dot(grad_pre_up, weight_up.T, preferred_element_type=jnp.float32)).astype(jnp.bfloat16)
    sum_gate = jnp.dot(rows_x.T, grad_pre_gate, preferred_element_type=jnp.float32).astype(jnp.bfloat16)
    sum_up = jnp.dot(rows_x.T, grad_pre_up, preferred_element_type=jnp.float32).astype(jnp.bfloat16)
    sum_down = jnp.dot(gated_hidden.T, rows_dy, preferred_element_type=jnp.float32).astype(jnp.bfloat16)
    return partial_out, partial_dx, sum_gate, sum_up, sum_down


def reference(tokens, grad_out, routes, gates, pull_list, counts, w_gate, w_up, w_down):
    group_rows = DEVICE_TOKENS * N_DEV
    row_count = N_DEV * SLOT_CEILING
    x_all = tokens.reshape(N_GROUP, group_rows, D)
    dy_all = grad_out.reshape(N_GROUP, group_rows, D)
    route_all = routes.reshape(N_GROUP, group_rows * CHOSEN_EXPERTS)
    gate_all = gates.reshape(N_GROUP, group_rows * CHOSEN_EXPERTS)
    live_rows = jnp.arange(group_rows)[None, :] < counts[:, None]
    valid_all = jnp.repeat(live_rows, CHOSEN_EXPERTS, axis=1)
    gate_blocks = w_gate.reshape(EXPERTS, SLICES, D, H_DEV)
    up_blocks = w_up.reshape(EXPERTS, SLICES, D, H_DEV)
    down_blocks = w_down.reshape(EXPERTS, SLICES, H_DEV, D)

    def one_expert(carry, expert_id):
        out_acc, dx_acc = carry
        owner_group = expert_id // EXP_GROUP
        local_index = expert_id % EXP_GROUP
        taker_group = (owner_group + 1) % N_GROUP
        borrowed_match = pull_list[taker_group] == expert_id
        is_pulled = jnp.any(borrowed_match)
        pull_slot = EXP_GROUP + jnp.sum(jnp.where(borrowed_match, jnp.arange(PULL), 0))
        shares = []
        for group_index, slot_index, enabled in ((owner_group, local_index, True), (taker_group, pull_slot, is_pulled)):
            matched = (route_all[group_index] == slot_index) & valid_all[group_index] & enabled
            match_count = jnp.sum(matched.astype(jnp.int32))
            pair_index = jnp.nonzero(matched, size=row_count, fill_value=0)[0].astype(jnp.int32)
            is_live = jnp.arange(row_count) < match_count
            token_index = (pair_index // CHOSEN_EXPERTS).astype(jnp.int32)
            rows_x = x_all[group_index][token_index]
            rows_dy = dy_all[group_index][token_index]
            rows_gate = jnp.where(is_live, gate_all[group_index][pair_index], jnp.zeros((), gates.dtype))
            per_slice = []
            for slice_index in range(SLICES):
                result = expert_pass(rows_x, rows_dy, rows_gate, gate_blocks[expert_id, slice_index],
                                     up_blocks[expert_id, slice_index], down_blocks[expert_id, slice_index])
                out_acc = out_acc.at[group_index, token_index].add(result[0].astype(jnp.float32))
                dx_acc = dx_acc.at[group_index, token_index].add(result[1].astype(jnp.float32))
                per_slice.append(result[2:])
            shares.append(per_slice)
        outputs = []
        for which in range(3):
            stacked = [(shares[0][slice_index][which].astype(jnp.float32)
                        + shares[1][slice_index][which].astype(jnp.float32)).astype(jnp.bfloat16)
                       for slice_index in range(SLICES)]
            outputs.append(jnp.stack(stacked))
        return (out_acc, dx_acc), tuple(outputs)

    start = (jnp.zeros((N_GROUP, group_rows, D), jnp.float32), jnp.zeros((N_GROUP, group_rows, D), jnp.float32))
    (out_acc, dx_acc), (grad_g, grad_u, grad_d) = lax.scan(one_expert, start, jnp.arange(EXPERTS))
    mixed = out_acc.reshape(TOKEN_ROWS_ALL, D).astype(jnp.bfloat16)
    token_grad = dx_acc.reshape(TOKEN_ROWS_ALL, D).astype(jnp.bfloat16)
    return (mixed, token_grad, grad_g.reshape(EXPERTS * SLICES, D, H_DEV),
            grad_u.reshape(EXPERTS * SLICES, D, H_DEV), grad_d.reshape(EXPERTS * SLICES, H_DEV, D))
```

```python
import jax
import jax.numpy as jnp
from jax import lax
from jax.experimental import pallas as pl
from jax.experimental.pallas import tpu as pltpu
from jax.sharding import PartitionSpec as P

BF = jnp.bfloat16
F32 = jnp.float32
D = 2560
H = 384
ROWS = 16
CAP = 6
NX, NY, NZ = 4, 4, 8
META = 128
GATE_LANE = 64
BLK = NZ * CAP
HALF = NX * BLK
ALL = 2 * HALF
TOK = NZ * ROWS
STEP = 512
MESH = pl.DeviceIdType.MESH


def nn(a, b):
    return lax.dot_general(a, b, (((1,), (0,)), ((), ())), preferred_element_type=F32)


def nt(a, b):
    return lax.dot_general(a, b, (((1,), (1,)), ((), ())), preferred_element_type=F32)


def tn(a, b):
    return lax.dot_general(a, b, (((0,), (0,)), ((), ())), preferred_element_type=F32)


def rows(i, n):
    return pl.ds(pl.multiple_of(i * n, n), n)


def over_lanes(body):
    def run(i, carry):
        body(pl.ds(pl.multiple_of(i * STEP, STEP), STEP))
        return carry

    lax.fori_loop(0, D // STEP, run, 0)


def kernel(
    tokens, grad_out, meta_in, wg_hbm, wu_hbm, wd_hbm,
    mixed, token_grad, gg_hbm, gu_hbm, gd_hbm,
    bx, bdy, sx, sdy, rx, rdy, wg, wu, wd, sel, sel_gate,
    act, slope, hid, gpre, part, out_far, dx_far, out_in, dx_in,
    out_back, dx_back, out_got, dx_got, pout, pdx, zout, zdx, gg, gu, gd,
    w_sem, z_send, z_recv, x_send, x_recv, c_send, c_recv,
    e_send, e_recv, b_send, b_recv, p_send, p_recv, g_sem,
):
    g = lax.axis_index("group")
    d = lax.axis_index("dev")
    y, z_lo = g // 2, g % 2
    z_hi, x, c = d // 8, (d // 2) % 4, d % 2
    z = z_hi * 2 + z_lo

    def device(x_, y_, z_, c_):
        return (y_ * 2 + z_ % 2, ((z_ // 2) * NX + x_) * 2 + c_)

    y_prev = jnp.where(z_lo == 1, y, (y + NY - 1) % NY)
    y_next = jnp.where(z_lo == 0, y, (y + 1) % NY)

    def z_taker(k):
        return device(x, y if k % 2 == 0 else y_prev, (z + k) % NZ, c)

    def z_owner(k):
        return device(x, y if k % 2 == 0 else y_next, (z + k) % NZ, c)

    sibling = device(x, y, z, 1 - c)

    w_copies = [
        pltpu.make_async_copy(src.at[0], dst, w_sem.at[i])
        for i, (src, dst) in enumerate(((wg_hbm, wg), (wu_hbm, wu), (wd_hbm, wd)))
    ]
    for copy in w_copies:
        copy.start()

    barrier = pltpu.get_barrier_semaphore()
    near = [z_taker(k) for k in range(1, NZ)] + [z_owner(k) for k in range(1, NZ, 2)]
    near += [device((x + k) % NX, y, z, c) for k in range(1, NX)] + [sibling]
    for other in near:
        pl.semaphore_signal(barrier, inc=1, device_id=other, device_id_type=MESH)
    mine = rows(z, ROWS)
    bx[mine, :D] = tokens[...]
    bx[mine, D:] = meta_in[...]
    bdy[mine, :] = grad_out[...]
    pl.semaphore_wait(barrier, len(near))

    sent = []

    def send(src, dst, s_sem, r_sem, to):
        copy = pltpu.make_async_remote_copy(
            src_ref=src, dst_ref=dst, send_sem=s_sem, recv_sem=r_sem,
            device_id=to, device_id_type=MESH,
        )
        copy.start()
        sent.append(copy)

    def arrived(dst, s_sem, r_sem):
        pltpu.make_async_remote_copy(
            src_ref=dst, dst_ref=dst, send_sem=s_sem, recv_sem=r_sem,
            device_id=sibling, device_id_type=MESH,
        ).wait_recv()

    far_first = (4, 3, 5, 2, 6, 1, 7)
    for s, buf in enumerate((bx, bdy)):
        for k in far_first:
            send(buf.at[mine], buf.at[mine], z_send.at[s, k], z_recv.at[s, z], z_taker(k))

    def z_arrived(s, buf):
        for k in range(1, NZ):
            zz = (z + k) % NZ
            arrived(buf.at[rows(zz, ROWS)], z_send.at[s, 0], z_recv.at[s, zz])

    z_arrived(0, bx)
    meta = bx[:, D:].astype(F32)
    lane = lax.broadcasted_iota(jnp.int32, (TOK, META), 1)
    gate_at = pltpu.roll(meta, GATE_LANE, 1)
    first = (g * 16 + z_hi * NX).astype(F32)
    hits, gate_of = [], []
    hit_all = jnp.zeros((TOK, META), F32)
    for j in range(NX):
        match = jnp.where((meta == first + j) & (lane < 6), 1.0, 0.0)
        hits.append(jnp.sum(match, axis=1, keepdims=True))
        gate_of.append(jnp.sum(match * gate_at, axis=1, keepdims=True))
        hit_all = hit_all + jnp.where(lane == j, hits[j], 0.0)
    t_row = lax.broadcasted_iota(jnp.int32, (TOK, TOK), 0)
    t_col = lax.broadcasted_iota(jnp.int32, (TOK, TOK), 1)
    before = jnp.where((t_col < t_row) & (t_col // ROWS == t_row // ROWS), 1.0, 0.0)
    rank_all = nn(before.astype(BF), hit_all.astype(BF))
    q = lax.broadcasted_iota(jnp.int32, (TOK, HALF), 1)
    block = lax.broadcasted_iota(jnp.int32, (TOK, HALF), 0) // ROWS
    place = jnp.zeros((TOK, HALF), F32)
    hit_q = jnp.zeros((TOK, HALF), F32)
    gate_q = jnp.zeros((TOK, HALF), F32)
    for j in range(NX):
        rank = jnp.sum(jnp.where(lane == j, rank_all, 0.0), axis=1, keepdims=True)
        inside = (q >= j * BLK) & (q < (j + 1) * BLK)
        place = jnp.where(inside, rank + j * BLK, place)
        hit_q = jnp.where(inside, hits[j], hit_q)
        gate_q = jnp.where(inside, gate_of[j], gate_q)
    placed = place + (block * CAP).astype(F32) == q.astype(F32)
    chosen = jnp.where(placed, hit_q, 0.0)
    sel[...] = chosen.astype(BF)
    sel_gate[...] = (chosen * gate_q).astype(BF)

    my_slot = rows(c * NX + x, BLK)

    def dispatch(s, selector, buf, out, got):
        def body(at):
            out[:, at] = tn(selector[...], buf[:, at]).astype(BF)

        over_lanes(body)
        for k in (2, 1, 3):
            j = (x + k) % NX
            send(out.at[rows(j, BLK)], got.at[my_slot], x_send.at[s, k], x_recv.at[s, x], device(j, y, z, c))
        got[my_slot, :] = out[rows(x, BLK), :]
        send(got.at[my_slot], got.at[my_slot], c_send.at[s, 0], c_recv.at[s, x], sibling)

    def share(s, got):
        for k in (1, 3, 2):
            j = (x + k) % NX
            slot = got.at[rows(c * NX + j, BLK)]
            arrived(slot, x_send.at[s, 0], x_recv.at[s, j])
            send(slot, slot, c_send.at[s, k], c_recv.at[s, j], sibling)

    def shared(s, got):
        for k in range(NX):
            j = (x + k) % NX
            arrived(got.at[rows((1 - c) * NX + j, BLK)], c_send.at[s, 0], c_recv.at[s, j])

    dispatch(0, sel, bx, sx, rx)
    z_arrived(1, bdy)
    dispatch(1, sel_gate, bdy, sdy, rdy)
    share(0, rx)
    shared(0, rx)

    far_rows, own_rows = rows(1 - c, HALF), rows(c, HALF)

    w_copies[0].wait()
    w_copies[1].wait()
    pre_gate = nn(rx[...], wg[...])
    pre_up = nn(rx[...], wu[...])
    sig = jax.nn.sigmoid(pre_gate)
    silu = pre_gate * sig
    act[...] = silu
    slope[...] = pre_up * sig * (1.0 + pre_gate * (1.0 - sig))
    hid[...] = (silu * pre_up).astype(BF)
    w_copies[2].wait()

    def back(s, rows_of, far, near_in, summed, got):
        def body_far(at):
            far[:, at] = rows_of(far_rows, at).astype(BF)

        over_lanes(body_far)
        send(far, near_in, e_send.at[s], e_recv.at[s], sibling)

        def body_own(at):
            part[:, at] = rows_of(own_rows, at)

        over_lanes(body_own)

    def give_back(s, near_in, summed, got):
        arrived(near_in, e_send.at[s], e_recv.at[s])
        summed[...] = (part[...] + near_in[...].astype(F32)).astype(BF)
        for k in (2, 1, 3):
            j = (x + k) % NX
            send(summed.at[rows(j, BLK)], got.at[rows(x, BLK)], b_send.at[s, k], b_recv.at[s, x], device(j, y, z, c))
        got[rows(x, BLK), :] = summed[rows(x, BLK), :]

    def combine(s, selector, got, partial, landed):
        for k in range(1, NX):
            j = (x + k) % NX
            arrived(got.at[rows(j, BLK)], b_send.at[s, 0], b_recv.at[s, j])

        def body(at):
            partial[:, at] = nn(selector[...], got[:, at]).astype(BF)

        over_lanes(body)
        for k in far_first:
            send(partial.at[rows((z + k) % NZ, ROWS)], landed.at[mine], p_send.at[s, k], p_recv.at[s, z], z_owner(k))
        landed[mine, :] = partial[mine, :]

    def finish(s, landed, result):
        for k in range(1, NZ):
            zz = (z + k) % NZ
            arrived(landed.at[rows(zz, ROWS)], p_send.at[s, 0], p_recv.at[s, zz])
        total = landed[:ROWS, :].astype(F32)
        for i in range(1, NZ):
            total = total + landed[i * ROWS:(i + 1) * ROWS, :].astype(F32)
        result[...] = total.astype(BF)

    back(0, lambda r, at: nn(hid[r, :], wd[:, at]), out_far, out_in, out_back, out_got)
    share(1, rdy)
    give_back(0, out_in, out_back, out_got)
    shared(1, rdy)

    back_hidden = nt(rdy[...], wd[...])
    gpre[:, :H] = (back_hidden * slope[...]).astype(BF)
    gpre[:, H:] = (back_hidden * act[...]).astype(BF)
    back(
        1,
        lambda r, at: nt(gpre[r, :H], wg[at, :]) + nt(gpre[r, H:], wu[at, :]),
        dx_far, dx_in, dx_back, dx_got,
    )
    combine(0, sel_gate, out_got, pout, zout)
    give_back(1, dx_in, dx_back, dx_got)

    def grads_in(at):
        both = tn(rx[:, at], gpre[...])
        gg[at, :] = both[:, :H].astype(BF)
        gu[at, :] = both[:, H:].astype(BF)

    over_lanes(grads_in)

    def grads_down(at):
        gd[:, at] = tn(hid[...], rdy[:, at]).astype(BF)

    over_lanes(grads_down)
    g_copies = [
        pltpu.make_async_copy(src, dst.at[0], g_sem.at[i])
        for i, (src, dst) in enumerate(((gg, gg_hbm), (gu, gu_hbm), (gd, gd_hbm)))
    ]
    for copy in g_copies:
        copy.start()
    combine(1, sel, dx_got, pdx, zdx)
    finish(0, zout, mixed)
    finish(1, zdx, token_grad)
    for copy in sent:
        copy.wait_send()
    for copy in g_copies:
        copy.wait()


def shards(tokens, grad_out, routes, gates, pull_list, counts, w_gate, w_up, w_down):
    g = lax.axis_index("group")
    d = lax.axis_index("dev")
    n_pull = pull_list.shape[1]
    mine = jnp.arange(pull_list.shape[0]) == g
    pull_row = jnp.sum(jnp.where(mine[:, None], pull_list, 0), axis=0)
    count = jnp.sum(jnp.where(mine, counts, 0))
    pulled = routes[:, :, None] == 16 + jnp.arange(n_pull)[None, None, :]
    expert = jnp.where(
        routes < 16, g * 16 + routes, jnp.sum(jnp.where(pulled, pull_row[None, None, :], 0), axis=2)
    )
    alive = d * ROWS + jnp.arange(ROWS) < count
    expert = jnp.where(alive[:, None], expert, -1)
    gap = jnp.zeros((ROWS, GATE_LANE - routes.shape[1]), BF)
    meta = jnp.concatenate([expert.astype(BF), gap, gates, gap], axis=1)

    vmem = pl.BlockSpec(memory_space=pltpu.VMEM)
    hbm = pl.BlockSpec(memory_space=pl.ANY)
    dma = pltpu.SemaphoreType.DMA
    return pl.pallas_call(
        kernel,
        out_shape=(
            jax.ShapeDtypeStruct((ROWS, D), BF),
            jax.ShapeDtypeStruct((ROWS, D), BF),
            jax.ShapeDtypeStruct((1, D, H), BF),
            jax.ShapeDtypeStruct((1, D, H), BF),
            jax.ShapeDtypeStruct((1, H, D), BF),
        ),
        in_specs=[vmem] * 3 + [hbm] * 3,
        out_specs=(vmem, vmem, hbm, hbm, hbm),
        scratch_shapes=[
            pltpu.VMEM((TOK, D + META), BF),
            pltpu.VMEM((TOK, D), BF),
            pltpu.VMEM((HALF, D), BF),
            pltpu.VMEM((HALF, D), BF),
            pltpu.VMEM((ALL, D), BF),
            pltpu.VMEM((ALL, D), BF),
            pltpu.VMEM((D, H), BF),
            pltpu.VMEM((D, H), BF),
            pltpu.VMEM((H, D), BF),
            pltpu.VMEM((TOK, HALF), BF),
            pltpu.VMEM((TOK, HALF), BF),
            pltpu.VMEM((ALL, H), F32),
            pltpu.VMEM((ALL, H), F32),
            pltpu.VMEM((ALL, H), BF),
            pltpu.VMEM((ALL, 2 * H), BF),
            pltpu.VMEM((HALF, D), F32),
            pltpu.VMEM((HALF, D), BF),
            pltpu.VMEM((HALF, D), BF),
            pltpu.VMEM((HALF, D), BF),
            pltpu.VMEM((HALF, D), BF),
            pltpu.VMEM((HALF, D), BF),
            pltpu.VMEM((HALF, D), BF),
            pltpu.VMEM((HALF, D), BF),
            pltpu.VMEM((HALF, D), BF),
            pltpu.VMEM((TOK, D), BF),
            pltpu.VMEM((TOK, D), BF),
            pltpu.VMEM((TOK, D), BF),
            pltpu.VMEM((TOK, D), BF),
            pltpu.VMEM((D, H), BF),
            pltpu.VMEM((D, H), BF),
            pltpu.VMEM((H, D), BF),
            dma((3,)),
            dma((2, NZ)),
            dma((2, NZ)),
            dma((2, NX)),
            dma((2, NX)),
            dma((2, NX)),
            dma((2, NX)),
            dma((2,)),
            dma((2,)),
            dma((2, NX)),
            dma((2, NX)),
            dma((2, NZ)),
            dma((2, NZ)),
            dma((3,)),
        ],
        compiler_params=pltpu.CompilerParams(
            collective_id=0, has_side_effects=True, vmem_limit_bytes=56 * 1024 * 1024
        ),
    )(tokens, grad_out, meta, w_gate, w_up, w_down)


def solution(mesh):
    both = ("group", "dev")
    in_specs = (
        P(both, None), P(both, None), P(both, None), P(both, None), P(), P(),
        P(both, None, None), P(both, None, None), P(both, None, None),
    )
    out_specs = (
        P(both, None), P(both, None),
        P(both, None, None), P(both, None, None), P(both, None, None),
    )
    return jax.shard_map(shards, mesh=mesh, in_specs=in_specs, out_specs=out_specs, check_vma=False)
```

```python
import jax
import jax.numpy as jnp
from jax import lax
from jax.experimental import pallas as pl
from jax.experimental.pallas import tpu as pltpu
from jax.sharding import PartitionSpec as P

BF = jnp.bfloat16
F32 = jnp.float32
D = 2560
H = 384
ROWS = 16
CAP = 6
NX, NY, NZ = 4, 4, 8
META = 128
GATE_LANE = 64
BLK = NZ * CAP
HALF = NX * BLK
ALL = 2 * HALF
TOK = NZ * ROWS
STEP = 512
MESH = pl.DeviceIdType.MESH


def nn(a, b):
    return lax.dot_general(a, b, (((1,), (0,)), ((), ())), preferred_element_type=F32)


def nt(a, b):
    return lax.dot_general(a, b, (((1,), (1,)), ((), ())), preferred_element_type=F32)


def tn(a, b):
    return lax.dot_general(a, b, (((0,), (0,)), ((), ())), preferred_element_type=F32)


def rows(i, n):
    return pl.ds(pl.multiple_of(i * n, n), n)


def over_lanes(body):
    def run(i, carry):
        body(pl.ds(pl.multiple_of(i * STEP, STEP), STEP))
        return carry

    lax.fori_loop(0, D // STEP, run, 0)


def kernel(
    tokens, grad_out, routes_hbm, gates_hbm, pull_hbm, counts_hbm, wg_hbm, wu_hbm, wd_hbm,
    mixed, token_grad, gg_hbm, gu_hbm, gd_hbm,
    bx, bdy, sx, sdy, rx, rdy, wg, wu, wd, sel, sel_gate,
    act, slope, hid, gpre, part, out_far, dx_far, out_in, dx_in,
    out_back, dx_back, out_got, dx_got, pout, pdx, zout, zdx, gg, gu, gd,
    routes, gates, pull_list, counts, chosen_t, w_sem, t_sem, z_send, z_recv, y_send, y_recv, x_send, x_recv, c_send, c_recv,
    e_send, e_recv, b_send, b_recv, p_send, p_recv, g_sem,
):
    g = lax.axis_index("group")
    d = lax.axis_index("dev")
    y, z_lo = g // 2, g % 2
    z_hi, x, c = d // 8, (d // 2) % 4, d % 2
    z = z_hi * 2 + z_lo

    def device(x_, y_, z_, c_):
        return (y_ * 2 + z_ % 2, ((z_ // 2) * NX + x_) * 2 + c_)

    y_prev = jnp.where(z_lo == 1, y, (y + NY - 1) % NY)
    y_next = jnp.where(z_lo == 0, y, (y + 1) % NY)

    def z_taker(k):
        return device(x, y if k % 2 == 0 else y_prev, (z + k) % NZ, c)

    def z_owner(k):
        return device(x, y if k % 2 == 0 else y_next, (z + k) % NZ, c)

    sibling = device(x, y, z, 1 - c)

    barrier = pltpu.get_barrier_semaphore()
    near = [z_taker(k) for k in range(1, NZ)] + [z_owner(k) for k in range(1, NZ, 2)]
    near += [device((x + k) % NX, y, z, c) for k in range(1, NX)] + [sibling]
    for other in near:
        pl.semaphore_signal(barrier, inc=1, device_id=other, device_id_type=MESH)
    mine = rows(z, ROWS)
    t_copies = [
        pltpu.make_async_copy(tokens, bx.at[mine, :D], t_sem.at[0]),
        pltpu.make_async_copy(grad_out, bdy.at[mine], t_sem.at[1]),
    ]
    r_copies = [
        pltpu.make_async_copy(src, dst, t_sem.at[2 + i])
        for i, (src, dst) in enumerate(
            ((routes_hbm, routes), (gates_hbm, gates), (pull_hbm, pull_list), (counts_hbm, counts))
        )
    ]
    w_copies = [
        pltpu.make_async_copy(src.at[0], dst, w_sem.at[i])
        for i, (src, dst) in enumerate(((wg_hbm, wg), (wu_hbm, wu), (wd_hbm, wd)))
    ]
    for copy in r_copies + t_copies + w_copies:
        copy.start()
    for copy in r_copies:
        copy.wait()

    route = routes[...]
    expert = g * 16 + route
    for j in range(8):
        expert = jnp.where(route == 16 + j, pull_list[g, j], expert)
    token = d * ROWS + lax.broadcasted_iota(jnp.int32, route.shape, 1)
    expert = jnp.where(token < counts[g], expert, -1)
    chosen_t[...] = jnp.zeros_like(chosen_t)
    chosen_t[:6, :] = expert.astype(F32)
    chosen_t[8:14, :] = gates[...].astype(F32)
    k_row = lax.broadcasted_iota(jnp.int32, (ROWS, META), 0)
    k_lane = lax.broadcasted_iota(jnp.int32, (ROWS, META), 1)
    spread = (k_lane == k_row) & (k_row < 8) | (k_lane == k_row + (GATE_LANE - 8)) & (k_row >= 8)
    meta_in = tn(chosen_t[...].astype(BF), jnp.where(spread, 1.0, 0.0).astype(BF))
    bx[mine, D:] = meta_in.astype(BF)
    for copy in t_copies:
        copy.wait()
    pl.semaphore_wait(barrier, len(near))

    sent = []

    def send(src, dst, s_sem, r_sem, to):
        copy = pltpu.make_async_remote_copy(
            src_ref=src, dst_ref=dst, send_sem=s_sem, recv_sem=r_sem,
            device_id=to, device_id_type=MESH,
        )
        copy.start()
        sent.append(copy)

    def arrived(dst, s_sem, r_sem):
        pltpu.make_async_remote_copy(
            src_ref=dst, dst_ref=dst, send_sem=s_sem, recv_sem=r_sem,
            device_id=sibling, device_id_type=MESH,
        ).wait_recv()

    far_first = (4, 3, 5, 2, 6, 1, 7)
    buffers = (bx, bdy)
    ring = (device(x, y, (z + 1) % NZ, c), device(x, y, (z + NZ - 1) % NZ, c))
    y_back = device(x, (y + NY - 1) % NY, z, c)

    def slot(block, odd):
        return rows(jnp.where((odd == 1) & (block % 2 == 0), NZ + block // 2, block), ROWS)

    def lanes_of(s, way, step):
        width = buffers[s].shape[1]
        if step < 4:
            return pl.ds(0, width)
        return pl.ds(0, D // 2) if way == 0 else pl.ds(D // 2, width - D // 2)

    def ring_block(way, step):
        return (z + NZ - step) % NZ if way == 0 else (z + step) % NZ

    def pass_on(s, way, step):
        block, at = ring_block(way, step - 1), lanes_of(s, way, step)
        send(
            buffers[s].at[slot(block, z_lo), at], buffers[s].at[slot(block, 1 - z_lo), at],
            z_send.at[s, way, step], z_recv.at[s, way, step], ring[way],
        )

    def ring_arrived(s, way, step):
        at = lanes_of(s, way, step)
        arrived(
            buffers[s].at[slot(ring_block(way, step), z_lo), at],
            z_send.at[s, way, 0], z_recv.at[s, way, step],
        )

    def y_copy(s, way, step):
        block = ring_block(way, step)
        return pltpu.make_async_remote_copy(
            src_ref=buffers[s].at[slot(block, z_lo)], dst_ref=buffers[s].at[rows(block, ROWS)],
            send_sem=y_send.at[s, way, step // 2], recv_sem=y_recv.at[s, way, step // 2],
            device_id=y_back, device_id_type=MESH,
        )

    def z_arrived(s):
        for way in range(2):
            ring_arrived(s, way, 4)

        @pl.when(z_lo == 1)
        def _():
            for step in (1, 3):
                for way in range(2):
                    y_copy(s, way, step).wait_recv()

    for s in range(2):
        for way in range(2):
            pass_on(s, way, 1)
    for step in (1, 2, 3):
        for s in range(2):
            for way in range(2):
                ring_arrived(s, way, step)
                pass_on(s, way, step + 1)
                if step != 2:
                    pl.when(z_lo == 1)(lambda s=s, way=way, step=step: y_copy(s, way, step).start())

    z_arrived(0)
    meta = bx[:TOK, D:].astype(F32)
    lane = lax.broadcasted_iota(jnp.int32, (TOK, META), 1)
    gate_at = pltpu.roll(meta, GATE_LANE, 1)
    first = (g * 16 + z_hi * NX).astype(F32)
    hits, gate_of = [], []
    hit_all = jnp.zeros((TOK, META), F32)
    for j in range(NX):
        match = jnp.where((meta == first + j) & (lane < 6), 1.0, 0.0)
        hits.append(jnp.sum(match, axis=1, keepdims=True))
        gate_of.append(jnp.sum(match * gate_at, axis=1, keepdims=True))
        hit_all = hit_all + jnp.where(lane == j, hits[j], 0.0)
    t_row = lax.broadcasted_iota(jnp.int32, (TOK, TOK), 0)
    t_col = lax.broadcasted_iota(jnp.int32, (TOK, TOK), 1)
    before = jnp.where((t_col < t_row) & (t_col // ROWS == t_row // ROWS), 1.0, 0.0)
    rank_all = nn(before.astype(BF), hit_all.astype(BF))
    q = lax.broadcasted_iota(jnp.int32, (TOK, HALF), 1)
    block = lax.broadcasted_iota(jnp.int32, (TOK, HALF), 0) // ROWS
    place = jnp.zeros((TOK, HALF), F32)
    hit_q = jnp.zeros((TOK, HALF), F32)
    gate_q = jnp.zeros((TOK, HALF), F32)
    for j in range(NX):
        rank = jnp.sum(jnp.where(lane == j, rank_all, 0.0), axis=1, keepdims=True)
        inside = (q >= j * BLK) & (q < (j + 1) * BLK)
        place = jnp.where(inside, rank + j * BLK, place)
        hit_q = jnp.where(inside, hits[j], hit_q)
        gate_q = jnp.where(inside, gate_of[j], gate_q)
    placed = place + (block * CAP).astype(F32) == q.astype(F32)
    chosen = jnp.where(placed, hit_q, 0.0)
    sel[...] = chosen.astype(BF)
    sel_gate[...] = (chosen * gate_q).astype(BF)

    my_slot = rows(c * NX + x, BLK)

    def dispatch(s, selector, buf, out, got):
        def body(at):
            out[:, at] = tn(selector[...], buf[:TOK, at]).astype(BF)

        over_lanes(body)
        for k in (2, 1, 3):
            j = (x + k) % NX
            send(out.at[rows(j, BLK)], got.at[my_slot], x_send.at[s, k], x_recv.at[s, x], device(j, y, z, c))
        got[my_slot, :] = out[rows(x, BLK), :]
        send(got.at[my_slot], got.at[my_slot], c_send.at[s, 0], c_recv.at[s, x], sibling)

    def share(s, got):
        for k in (1, 3, 2):
            j = (x + k) % NX
            slot = got.at[rows(c * NX + j, BLK)]
            arrived(slot, x_send.at[s, 0], x_recv.at[s, j])
            send(slot, slot, c_send.at[s, k], c_recv.at[s, j], sibling)

    def shared(s, got):
        for k in range(NX):
            j = (x + k) % NX
            arrived(got.at[rows((1 - c) * NX + j, BLK)], c_send.at[s, 0], c_recv.at[s, j])

    dispatch(0, sel, bx, sx, rx)
    z_arrived(1)
    dispatch(1, sel_gate, bdy, sdy, rdy)
    share(0, rx)
    shared(0, rx)

    far_rows, own_rows = rows(1 - c, HALF), rows(c, HALF)

    w_copies[0].wait()
    w_copies[1].wait()
    pre_gate = nn(rx[...], wg[...])
    pre_up = nn(rx[...], wu[...])
    sig = jax.nn.sigmoid(pre_gate)
    silu = pre_gate * sig
    act[...] = silu
    slope[...] = pre_up * sig * (1.0 + pre_gate * (1.0 - sig))
    hid[...] = (silu * pre_up).astype(BF)
    w_copies[2].wait()

    def back(s, rows_of, far, near_in, summed, got):
        def body_far(at):
            far[:, at] = rows_of(far_rows, at).astype(BF)

        over_lanes(body_far)
        send(far, near_in, e_send.at[s], e_recv.at[s], sibling)

        def body_own(at):
            part[:, at] = rows_of(own_rows, at)

        over_lanes(body_own)

    def give_back(s, near_in, summed, got):
        arrived(near_in, e_send.at[s], e_recv.at[s])
        summed[...] = (part[...] + near_in[...].astype(F32)).astype(BF)
        for k in (2, 1, 3):
            j = (x + k) % NX
            send(summed.at[rows(j, BLK)], got.at[rows(x, BLK)], b_send.at[s, k], b_recv.at[s, x], device(j, y, z, c))
        got[rows(x, BLK), :] = summed[rows(x, BLK), :]

    def combine(s, selector, got, partial, landed):
        for k in range(1, NX):
            j = (x + k) % NX
            arrived(got.at[rows(j, BLK)], b_send.at[s, 0], b_recv.at[s, j])

        def body(at):
            partial[:, at] = nn(selector[...], got[:, at]).astype(BF)

        over_lanes(body)
        for k in far_first:
            send(partial.at[rows((z + k) % NZ, ROWS)], landed.at[mine], p_send.at[s, k], p_recv.at[s, z], z_owner(k))
        landed[mine, :] = partial[mine, :]

    def finish(s, landed, result):
        for k in range(1, NZ):
            zz = (z + k) % NZ
            arrived(landed.at[rows(zz, ROWS)], p_send.at[s, 0], p_recv.at[s, zz])
        total = landed[:ROWS, :].astype(F32)
        for i in range(1, NZ):
            total = total + landed[i * ROWS:(i + 1) * ROWS, :].astype(F32)
        result[...] = total.astype(BF)

    back(0, lambda r, at: nn(hid[r, :], wd[:, at]), out_far, out_in, out_back, out_got)
    share(1, rdy)
    give_back(0, out_in, out_back, out_got)
    shared(1, rdy)

    back_hidden = nt(rdy[...], wd[...])
    gpre[:, :H] = (back_hidden * slope[...]).astype(BF)
    gpre[:, H:] = (back_hidden * act[...]).astype(BF)
    back(
        1,
        lambda r, at: nt(gpre[r, :H], wg[at, :]) + nt(gpre[r, H:], wu[at, :]),
        dx_far, dx_in, dx_back, dx_got,
    )
    combine(0, sel_gate, out_got, pout, zout)
    give_back(1, dx_in, dx_back, dx_got)

    def grads_in(at):
        both = tn(rx[:, at], gpre[...])
        gg[at, :] = both[:, :H].astype(BF)
        gu[at, :] = both[:, H:].astype(BF)

    over_lanes(grads_in)

    def grads_down(at):
        gd[:, at] = tn(hid[...], rdy[:, at]).astype(BF)

    over_lanes(grads_down)
    g_copies = [
        pltpu.make_async_copy(src, dst.at[0], g_sem.at[i])
        for i, (src, dst) in enumerate(((gg, gg_hbm), (gu, gu_hbm), (gd, gd_hbm)))
    ]
    for copy in g_copies:
        copy.start()
    combine(1, sel, dx_got, pdx, zdx)
    finish(0, zout, mixed)
    finish(1, zdx, token_grad)
    for copy in sent:
        copy.wait_send()

    @pl.when(z_lo == 1)
    def _():
        for s in range(2):
            for way in range(2):
                for step in (1, 3):
                    y_copy(s, way, step).wait_send()

    for copy in g_copies:
        copy.wait()


def copy_kernel(*refs):
    n = (len(refs) - 1) // 2
    sems = refs[-1]
    copies = []
    for i in range(n):
        src, dst = refs[i], refs[n + i]
        if len(src.shape) == 2:
            copies.append(pltpu.make_async_copy(src, dst, sems.at[i, 0]))
            continue
        part = src.shape[1] // 4
        for j in range(4):
            at = pl.ds(j * part, part)
            copies.append(pltpu.make_async_copy(src.at[0, at], dst.at[0, at], sems.at[i, j]))
    for copy in copies:
        copy.start()
    for copy in copies:
        copy.wait()


def shards(tokens, grad_out, routes, gates, pull_list, counts, w_gate, w_up, w_down):
    vmem = pl.BlockSpec(memory_space=pltpu.VMEM)
    hbm = pl.BlockSpec(memory_space=pl.ANY)
    dma = pltpu.SemaphoreType.DMA
    results = pl.pallas_call(
        kernel,
        out_shape=(
            pltpu.VMEM((ROWS, D), BF),
            pltpu.VMEM((ROWS, D), BF),
            pltpu.VMEM((1, D, H), BF),
            pltpu.VMEM((1, D, H), BF),
            pltpu.VMEM((1, H, D), BF),
        ),
        in_specs=[pl.BlockSpec(memory_space=pltpu.HBM)] * 9,
        out_specs=(vmem, vmem, hbm, hbm, hbm),
        scratch_shapes=[
            pltpu.VMEM((TOK + TOK // 2, D + META), BF),
            pltpu.VMEM((TOK + TOK // 2, D), BF),
            pltpu.VMEM((HALF, D), BF),
            pltpu.VMEM((HALF, D), BF),
            pltpu.VMEM((ALL, D), BF),
            pltpu.VMEM((ALL, D), BF),
            pltpu.VMEM((D, H), BF),
            pltpu.VMEM((D, H), BF),
            pltpu.VMEM((H, D), BF),
            pltpu.VMEM((TOK, HALF), BF),
            pltpu.VMEM((TOK, HALF), BF),
            pltpu.VMEM((ALL, H), F32),
            pltpu.VMEM((ALL, H), F32),
            pltpu.VMEM((ALL, H), BF),
            pltpu.VMEM((ALL, 2 * H), BF),
            pltpu.VMEM((HALF, D), F32),
            pltpu.VMEM((HALF, D), BF),
            pltpu.VMEM((HALF, D), BF),
            pltpu.VMEM((HALF, D), BF),
            pltpu.VMEM((HALF, D), BF),
            pltpu.VMEM((HALF, D), BF),
            pltpu.VMEM((HALF, D), BF),
            pltpu.VMEM((HALF, D), BF),
            pltpu.VMEM((HALF, D), BF),
            pltpu.VMEM((TOK, D), BF),
            pltpu.VMEM((TOK, D), BF),
            pltpu.VMEM((TOK, D), BF),
            pltpu.VMEM((TOK, D), BF),
            pltpu.VMEM((D, H), BF),
            pltpu.VMEM((D, H), BF),
            pltpu.VMEM((H, D), BF),
            pltpu.VMEM((6, ROWS), jnp.int32),
            pltpu.VMEM((6, ROWS), BF),
            pltpu.SMEM((8, 8), jnp.int32),
            pltpu.SMEM((8,), jnp.int32),
            pltpu.VMEM((ROWS, ROWS), F32),
            dma((3,)),
            dma((6,)),
            dma((2, 2, 5)),
            dma((2, 2, 5)),
            dma((2, 2, 2)),
            dma((2, 2, 2)),
            dma((2, NX)),
            dma((2, NX)),
            dma((2, NX)),
            dma((2, NX)),
            dma((2,)),
            dma((2,)),
            dma((2, NX)),
            dma((2, NX)),
            dma((2, NZ)),
            dma((2, NZ)),
            dma((3,)),
        ],
        compiler_params=pltpu.CompilerParams(
            collective_id=0, has_side_effects=True, vmem_limit_bytes=56 * 1024 * 1024
        ),
    )(tokens, grad_out, routes.T, gates.T, pull_list, counts, w_gate, w_up, w_down)
    return pl.pallas_call(
        copy_kernel,
        out_shape=tuple(jax.ShapeDtypeStruct(r.shape, r.dtype) for r in results),
        in_specs=[hbm] * 5,
        out_specs=(hbm,) * 5,
        scratch_shapes=[dma((5, 4))],
        compiler_params=pltpu.CompilerParams(vmem_limit_bytes=8 * 1024 * 1024),
    )(*results)


def solution(mesh):
    both = ("group", "dev")
    in_specs = (
        P(both, None), P(both, None), P(both, None), P(both, None), P(), P(),
        P(both, None, None), P(both, None, None), P(both, None, None),
    )
    out_specs = (
        P(both, None), P(both, None),
        P(both, None, None), P(both, None, None), P(both, None, None),
    )
    return jax.shard_map(shards, mesh=mesh, in_specs=in_specs, out_specs=out_specs, check_vma=False)
```

```python
import jax
import jax.numpy as jnp
from jax import lax
from jax.experimental import pallas as pl
from jax.experimental.pallas import tpu as pltpu
from jax.sharding import PartitionSpec as P

BF = jnp.bfloat16
F32 = jnp.float32
D = 2560
H = 384
ROWS = 16
CAP = 6
NX, NY, NZ = 4, 4, 8
META = 128
GATE_LANE = 64
BLK = NZ * CAP
HALF = NX * BLK
ALL = 2 * HALF
TOK = NZ * ROWS
HOPS = 4
GATHER = 1280
OUT_W, DX_W = 1280, 640
MESH = pl.DeviceIdType.MESH


def nn(a, b):
    return lax.dot_general(a, b, (((1,), (0,)), ((), ())), preferred_element_type=F32)


def nt(a, b):
    return lax.dot_general(a, b, (((1,), (1,)), ((), ())), preferred_element_type=F32)


def tn(a, b):
    return lax.dot_general(a, b, (((0,), (0,)), ((), ())), preferred_element_type=F32)


def rows(i, n):
    return pl.ds(pl.multiple_of(i * n, n), n)


def kernel(
    tokens, grad_out, routes_hbm, gates_hbm, pull_hbm, counts_hbm, wg_hbm, wu_hbm, wd_hbm,
    mixed, token_grad, gg_hbm, gu_hbm, gd_hbm,
    bm, bx, bdy, sx, sdy, rx, rdy, wg, wu, wd, sel, sel_gate,
    act, slope, hid, gpre, part, far_out, far_dx, near_out, near_dx,
    back_out, back_dx, got_out, got_dx, pout, pdx, via_out, via_dx, end_out, end_dx, gg, gu, gd,
    routes, gates, pull_list, counts, chosen_t, w_sem, t_sem, z_send, z_recv, y_send, y_recv,
    x_send, x_recv, c_send, c_recv, e_send, e_recv, b_send, b_recv, a_send, a_recv, p_send, p_recv, g_sem,
):
    g = lax.axis_index("group")
    d = lax.axis_index("dev")
    y, z_lo = g // 2, g % 2
    z_hi, x, c = d // 8, (d // 2) % 4, d % 2
    z = z_hi * 2 + z_lo

    def device(x_, y_, z_, c_):
        return (y_ * 2 + z_ % 2, ((z_ // 2) * NX + x_) * 2 + c_)

    y_prev = jnp.where(z_lo == 1, y, (y + NY - 1) % NY)
    y_next = jnp.where(z_lo == 0, y, (y + 1) % NY)

    def z_taker(k):
        return device(x, y if k % 2 == 0 else y_prev, (z + k) % NZ, c)

    def z_owner(k):
        return device(x, y if k % 2 == 0 else y_next, (z + k) % NZ, c)

    sibling = device(x, y, z, 1 - c)
    y_back = device(x, (y + NY - 1) % NY, z, c)

    barrier = pltpu.get_barrier_semaphore()
    near = [z_taker(1), z_taker(7), z_owner(1), z_owner(7), z_taker(2), z_taker(6)]
    near += [y_back, device(x, (y + 1) % NY, z, c), sibling]
    near += [device((x + k) % NX, y, z, c) for k in range(1, NX)]
    for other in near:
        pl.semaphore_signal(barrier, inc=1, device_id=other, device_id_type=MESH)
    mine = rows(z, ROWS)
    r_copies = [
        pltpu.make_async_copy(src, dst, t_sem.at[2 + i])
        for i, (src, dst) in enumerate(
            ((routes_hbm, routes), (gates_hbm, gates), (pull_hbm, pull_list), (counts_hbm, counts))
        )
    ]
    t_copies = [
        pltpu.make_async_copy(tokens, bx.at[mine], t_sem.at[0]),
        pltpu.make_async_copy(grad_out, bdy.at[mine], t_sem.at[1]),
    ]
    w_copies = [
        pltpu.make_async_copy(src.at[0], dst, w_sem.at[i])
        for i, (src, dst) in enumerate(((wg_hbm, wg), (wu_hbm, wu), (wd_hbm, wd)))
    ]
    for copy in r_copies + t_copies:
        copy.start()
    for copy in r_copies:
        copy.wait()

    route = routes[...]
    expert = g * 16 + route
    for j in range(8):
        expert = jnp.where(route == 16 + j, pull_list[g, j], expert)
    token = d * ROWS + lax.broadcasted_iota(jnp.int32, route.shape, 1)
    expert = jnp.where(token < counts[g], expert, -1)
    chosen_t[...] = jnp.zeros_like(chosen_t)
    chosen_t[:6, :] = expert.astype(F32)
    chosen_t[8:14, :] = gates[...].astype(F32)
    k_row = lax.broadcasted_iota(jnp.int32, (ROWS, META), 0)
    k_lane = lax.broadcasted_iota(jnp.int32, (ROWS, META), 1)
    spread = (k_lane == k_row) & (k_row < 8) | (k_lane == k_row + (GATE_LANE - 8)) & (k_row >= 8)
    meta_in = tn(chosen_t[...].astype(BF), jnp.where(spread, 1.0, 0.0).astype(BF))
    bm[mine, :] = meta_in.astype(BF)
    for copy in t_copies:
        copy.wait()
    pl.semaphore_wait(barrier, len(near))

    sent = []

    def send(src, dst, s_sem, r_sem, to):
        copy = pltpu.make_async_remote_copy(
            src_ref=src, dst_ref=dst, send_sem=s_sem, recv_sem=r_sem,
            device_id=to, device_id_type=MESH,
        )
        copy.start()
        sent.append(copy)

    def arrived(dst, s_sem, r_sem):
        pltpu.make_async_remote_copy(
            src_ref=dst, dst_ref=dst, send_sem=s_sem, recv_sem=r_sem,
            device_id=sibling, device_id_type=MESH,
        ).wait_recv()

    pieces = [(bm, 0, META)]
    pieces += [(buf, lo, GATHER) for buf in (bx, bdy) for lo in range(0, D, GATHER)]
    n_lo = D // GATHER
    x_pieces, dy_pieces = list(range(1, 1 + n_lo)), list(range(1 + n_lo, 1 + 2 * n_lo))
    ring = (device(x, y, (z + 1) % NZ, c), device(x, y, (z + NZ - 1) % NZ, c))

    def slot(block, odd):
        return rows(jnp.where((odd == 1) & (block % 2 == 0), NZ + block // 2, block), ROWS)

    def ways(i, step):
        return (0,) if i == 0 and step == HOPS else (0, 1)

    def lanes_of(i, way, step):
        buf, lo, width = pieces[i]
        if step < HOPS or i == 0:
            return pl.ds(lo, width)
        return pl.ds(lo + way * (width // 2), width // 2)

    def ring_block(way, step):
        return (z + NZ - step) % NZ if way == 0 else (z + step) % NZ

    def pass_on(i, way, step):
        block, at, buf = ring_block(way, step - 1), lanes_of(i, way, step), pieces[i][0]
        send(
            buf.at[slot(block, z_lo), at], buf.at[slot(block, 1 - z_lo), at],
            z_send.at[i, way, step], z_recv.at[i, way, step], ring[way],
        )

    def ring_arrived(i, way, step):
        at = lanes_of(i, way, step)
        arrived(pieces[i][0].at[slot(ring_block(way, step), z_lo), at], z_send.at[i, way, 0], z_recv.at[i, way, step])

    def y_copy(i, way, step):
        block, at, buf = ring_block(way, step), lanes_of(i, way, 1), pieces[i][0]
        return pltpu.make_async_remote_copy(
            src_ref=buf.at[slot(block, z_lo), at], dst_ref=buf.at[rows(block, ROWS), at],
            send_sem=y_send.at[i, way, step // 2], recv_sem=y_recv.at[i, way, step // 2],
            device_id=y_back, device_id_type=MESH,
        )

    def start(i):
        for way in range(2):
            pass_on(i, way, 1)

    def relay(i, step):
        for way in range(2):
            ring_arrived(i, way, step)
            if way in ways(i, step + 1):
                pass_on(i, way, step + 1)
            if step != 2:
                pl.when(z_lo == 1)(lambda: y_copy(i, way, step).start())

    def gathered(i):
        for way in ways(i, HOPS):
            ring_arrived(i, way, HOPS)

        @pl.when(z_lo == 1)
        def _():
            for step in (1, 3):
                for way in range(2):
                    y_copy(i, way, step).wait_recv()

    start(0)
    for i in x_pieces:
        start(i)
    for copy in w_copies:
        copy.start()
    for i in [0] + x_pieces:
        relay(i, 1)
    for i in dy_pieces:
        start(i)
    for i in [0] + x_pieces:
        relay(i, 2)
    for i in dy_pieces:
        relay(i, 1)
    for i in [0] + x_pieces:
        relay(i, 3)
    for i in dy_pieces:
        relay(i, 2)

    gathered(0)
    meta = bm[:TOK, :].astype(F32)
    lane = lax.broadcasted_iota(jnp.int32, (TOK, META), 1)
    gate_at = pltpu.roll(meta, GATE_LANE, 1)
    first = (g * 16 + z_hi * NX).astype(F32)
    hits, gate_of = [], []
    hit_all = jnp.zeros((TOK, META), F32)
    for j in range(NX):
        match = jnp.where((meta == first + j) & (lane < 6), 1.0, 0.0)
        hits.append(jnp.sum(match, axis=1, keepdims=True))
        gate_of.append(jnp.sum(match * gate_at, axis=1, keepdims=True))
        hit_all = hit_all + jnp.where(lane == j, hits[j], 0.0)
    t_row = lax.broadcasted_iota(jnp.int32, (TOK, TOK), 0)
    t_col = lax.broadcasted_iota(jnp.int32, (TOK, TOK), 1)
    before = jnp.where((t_col < t_row) & (t_col // ROWS == t_row // ROWS), 1.0, 0.0)
    rank_all = nn(before.astype(BF), hit_all.astype(BF))
    q = lax.broadcasted_iota(jnp.int32, (TOK, HALF), 1)
    block = lax.broadcasted_iota(jnp.int32, (TOK, HALF), 0) // ROWS
    place = jnp.zeros((TOK, HALF), F32)
    hit_q = jnp.zeros((TOK, HALF), F32)
    gate_q = jnp.zeros((TOK, HALF), F32)
    for j in range(NX):
        rank = jnp.sum(jnp.where(lane == j, rank_all, 0.0), axis=1, keepdims=True)
        inside = (q >= j * BLK) & (q < (j + 1) * BLK)
        place = jnp.where(inside, rank + j * BLK, place)
        hit_q = jnp.where(inside, hits[j], hit_q)
        gate_q = jnp.where(inside, gate_of[j], gate_q)
    placed = place + (block * CAP).astype(F32) == q.astype(F32)
    chosen = jnp.where(placed, hit_q, 0.0)
    sel[...] = chosen.astype(BF)
    sel_gate[...] = (chosen * gate_q).astype(BF)

    my_slot = rows(c * NX + x, BLK)
    dests = {i: (sx, rx) for i in x_pieces} | {i: (sdy, rdy) for i in dy_pieces}

    def dispatch(i, selector):
        buf, lo, width = pieces[i]
        out, got = dests[i]
        at = pl.ds(lo, width)
        gathered(i)
        out[:, at] = tn(selector[...], buf[:TOK, at]).astype(BF)
        for k in (2, 1, 3):
            j = (x + k) % NX
            send(out.at[rows(j, BLK), at], got.at[my_slot, at], x_send.at[i, k], x_recv.at[i, x], device(j, y, z, c))
        got[my_slot, at] = out[rows(x, BLK), at]
        send(got.at[my_slot, at], got.at[my_slot, at], c_send.at[i, 0], c_recv.at[i, x], sibling)

    def share(i):
        at, got = pl.ds(pieces[i][1], GATHER), dests[i][1]
        for k in (1, 3, 2):
            j = (x + k) % NX
            here = got.at[rows(c * NX + j, BLK), at]
            arrived(here, x_send.at[i, 0], x_recv.at[i, j])
            send(here, here, c_send.at[i, k], c_recv.at[i, j], sibling)

    def shared(i):
        at, got = pl.ds(pieces[i][1], GATHER), dests[i][1]
        for k in range(NX):
            j = (x + k) % NX
            arrived(got.at[rows((1 - c) * NX + j, BLK), at], c_send.at[i, 0], c_recv.at[i, j])

    for i in x_pieces[:1]:
        dispatch(i, sel)
    for i in dy_pieces:
        relay(i, 3)
    for i in x_pieces[1:]:
        dispatch(i, sel)
    for i in dy_pieces:
        dispatch(i, sel_gate)

    for copy in w_copies:
        copy.wait()
    pre_gate, pre_up = act, slope
    for n, i in enumerate(x_pieces):
        share(i)
        shared(i)
        at = pl.ds(pieces[i][1], GATHER)
        by_gate, by_up = nn(rx[:, at], wg[at, :]), nn(rx[:, at], wu[at, :])
        pre_gate[...] = by_gate if n == 0 else pre_gate[...] + by_gate
        pre_up[...] = by_up if n == 0 else pre_up[...] + by_up
    v_gate, v_up = pre_gate[...], pre_up[...]
    sig = jax.nn.sigmoid(v_gate)
    silu = v_gate * sig
    hid[...] = (silu * v_up).astype(BF)
    act[...] = silu
    slope[...] = v_up * sig * (1.0 + v_gate * (1.0 - sig))

    far_rows, own_rows = rows(1 - c, HALF), rows(c, HALF)
    back_pieces = [(0, lo, OUT_W) for lo in range(0, D, OUT_W)] + [(1, lo, DX_W) for lo in range(0, D, DX_W)]
    n_out = D // OUT_W
    out_back, dx_back = list(range(n_out)), list(range(n_out, len(back_pieces)))
    buffers = (
        (far_out, near_out, back_out, got_out, pout, via_out, end_out),
        (far_dx, near_dx, back_dx, got_dx, pdx, via_dx, end_dx),
    )

    def rows_of(s, r, at):
        if s == 0:
            return nn(hid[r, :], wd[:, at])
        return nt(gpre[r, :H], wg[at, :]) + nt(gpre[r, H:], wu[at, :])

    def back(todo):
        for i in todo:
            s, lo, width = back_pieces[i]
            far, near_in = buffers[s][:2]
            at = pl.ds(lo, width)
            far[:, at] = rows_of(s, far_rows, at).astype(BF)
            send(far.at[:, at], near_in.at[:, at], e_send.at[i], e_recv.at[i], sibling)
        for i in todo:
            s, lo, width = back_pieces[i]
            at = pl.ds(lo, width)
            part[:, at] = rows_of(s, own_rows, at)

    def give_back(i):
        s, lo, width = back_pieces[i]
        _, near_in, summed, got = buffers[s][:4]
        at = pl.ds(lo, width)
        arrived(near_in.at[:, at], e_send.at[i], e_recv.at[i])
        summed[:, at] = (part[:, at] + near_in[:, at].astype(F32)).astype(BF)
        for k in (2, 1, 3):
            j = (x + k) % NX
            send(
                summed.at[rows(j, BLK), at], got.at[rows(x, BLK), at],
                b_send.at[i, k], b_recv.at[i, x], device(j, y, z, c),
            )
        got[rows(x, BLK), at] = summed[rows(x, BLK), at]

    def split(i, way):
        lo, width = back_pieces[i][1:]
        first_part = (width // 2 + 127) // 128 * 128
        return pl.ds(lo, first_part) if way == 0 else pl.ds(lo + first_part, width - first_part)

    def combine(i, selector):
        s, lo, width = back_pieces[i]
        got, partial, via = buffers[s][3:6]
        at = pl.ds(lo, width)
        for k in range(1, NX):
            j = (x + k) % NX
            arrived(got.at[rows(j, BLK), at], b_send.at[i, 0], b_recv.at[i, j])
        partial[:, at] = nn(selector[...], got[:, at]).astype(BF)
        middle = rows((z + 4) % NZ, ROWS)
        for way, k in ((0, 3), (1, 5)):
            to = z_owner(2 if way == 0 else 6)
            outer = rows((z + k) % NZ, ROWS)
            send(partial.at[outer, at], via.at[rows(way, ROWS), at], a_send.at[i, way, 0], a_recv.at[i, way, 0], to)
            half = split(i, way)
            send(partial.at[middle, half], via.at[rows(2 + way, ROWS), half], a_send.at[i, way, 1], a_recv.at[i, way, 1], to)

    def send_home(i):
        s, lo, width = back_pieces[i]
        partial, via, end = buffers[s][4:]
        at = pl.ds(lo, width)
        for way, k in ((0, 1), (1, 7)):
            outer, half = rows(way, ROWS), split(i, way)
            arrived(via.at[outer, at], a_send.at[i, way, 0], a_recv.at[i, way, 0])
            spot = rows((z + k) % NZ, ROWS)
            partial[spot, at] = (partial[spot, at].astype(F32) + via[outer, at].astype(F32)).astype(BF)
            send(partial.at[spot, at], end.at[rows(way, ROWS), at], p_send.at[i, way, 0], p_recv.at[i, way, 0], z_owner(k))
            inner = rows(2 + way, ROWS)
            arrived(via.at[inner, half], a_send.at[i, way, 1], a_recv.at[i, way, 1])
            spot = rows((z + 2 * k) % NZ, ROWS)
            partial[spot, half] = (partial[spot, half].astype(F32) + via[inner, half].astype(F32)).astype(BF)
            send(partial.at[spot, at], end.at[inner, at], p_send.at[i, way, 1], p_recv.at[i, way, 1], z_owner((2 * k) % NZ))

    def finish(i, result):
        s, lo, width = back_pieces[i]
        partial, _, end = buffers[s][4:]
        at = pl.ds(lo, width)
        total = partial[mine, at].astype(F32)
        for n in range(2):
            for way in range(2):
                there = rows(2 * n + way, ROWS)
                arrived(end.at[there, at], p_send.at[i, way, n], p_recv.at[i, way, n])
                total = total + end[there, at].astype(F32)
        result[:, at] = total.astype(BF)

    back(out_back)
    for i in out_back:
        give_back(i)
    back_hidden = jnp.zeros((ALL, H), F32)
    for i in dy_pieces:
        share(i)
        shared(i)
        at = pl.ds(pieces[i][1], GATHER)
        back_hidden = back_hidden + nt(rdy[:, at], wd[:, at])
    gpre[:, :H] = (back_hidden * slope[...]).astype(BF)
    gpre[:, H:] = (back_hidden * act[...]).astype(BF)
    back(dx_back)
    for i in dx_back:
        give_back(i)
    combine(out_back[0], sel_gate)

    for lo in range(0, D, 1280):
        at = pl.ds(lo, 1280)
        both = tn(rx[:, at], gpre[...])
        gg[at, :] = both[:, :H].astype(BF)
        gu[at, :] = both[:, H:].astype(BF)
        gd[:, at] = tn(hid[...], rdy[:, at]).astype(BF)
    g_copies = [
        pltpu.make_async_copy(src, dst.at[0], g_sem.at[i])
        for i, (src, dst) in enumerate(((gg, gg_hbm), (gu, gu_hbm), (gd, gd_hbm)))
    ]
    for copy in g_copies:
        copy.start()

    todo = [(i, sel_gate) for i in out_back[1:]] + [(i, sel) for i in dx_back]
    last = out_back[0]
    for i, selector in todo:
        combine(i, selector)
        send_home(last)
        last = i
    send_home(last)
    for i in out_back:
        finish(i, mixed)
    for i in dx_back:
        finish(i, token_grad)
    for copy in sent:
        copy.wait_send()

    @pl.when(z_lo == 1)
    def _():
        for i in range(len(pieces)):
            for way in range(2):
                for step in (1, 3):
                    y_copy(i, way, step).wait_send()

    for copy in g_copies:
        copy.wait()


def copy_kernel(*refs):
    n = (len(refs) - 1) // 2
    sems = refs[-1]
    copies = []
    for i in range(n):
        src, dst = refs[i], refs[n + i]
        if len(src.shape) == 2:
            copies.append(pltpu.make_async_copy(src, dst, sems.at[i, 0]))
            continue
        part = src.shape[1] // 4
        for j in range(4):
            at = pl.ds(j * part, part)
            copies.append(pltpu.make_async_copy(src.at[0, at], dst.at[0, at], sems.at[i, j]))
    for copy in copies:
        copy.start()
    for copy in copies:
        copy.wait()


def shards(tokens, grad_out, routes, gates, pull_list, counts, w_gate, w_up, w_down):
    vmem = pl.BlockSpec(memory_space=pltpu.VMEM)
    hbm = pl.BlockSpec(memory_space=pl.ANY)
    dma = pltpu.SemaphoreType.DMA
    n_gather = 1 + 2 * (D // GATHER)
    n_back = D // OUT_W + D // DX_W
    results = pl.pallas_call(
        kernel,
        out_shape=(
            pltpu.VMEM((ROWS, D), BF),
            pltpu.VMEM((ROWS, D), BF),
            pltpu.VMEM((1, D, H), BF),
            pltpu.VMEM((1, D, H), BF),
            pltpu.VMEM((1, H, D), BF),
        ),
        in_specs=[pl.BlockSpec(memory_space=pltpu.HBM)] * 9,
        out_specs=(vmem, vmem, hbm, hbm, hbm),
        scratch_shapes=[
            pltpu.VMEM((TOK + TOK // 2, META), BF),
            pltpu.VMEM((TOK + TOK // 2, D), BF),
            pltpu.VMEM((TOK + TOK // 2, D), BF),
            pltpu.VMEM((HALF, D), BF),
            pltpu.VMEM((HALF, D), BF),
            pltpu.VMEM((ALL, D), BF),
            pltpu.VMEM((ALL, D), BF),
            pltpu.VMEM((D, H), BF),
            pltpu.VMEM((D, H), BF),
            pltpu.VMEM((H, D), BF),
            pltpu.VMEM((TOK, HALF), BF),
            pltpu.VMEM((TOK, HALF), BF),
            pltpu.VMEM((ALL, H), F32),
            pltpu.VMEM((ALL, H), F32),
            pltpu.VMEM((ALL, H), BF),
            pltpu.VMEM((ALL, 2 * H), BF),
            pltpu.VMEM((HALF, D), F32),
            pltpu.VMEM((HALF, D), BF),
            pltpu.VMEM((HALF, D), BF),
            pltpu.VMEM((HALF, D), BF),
            pltpu.VMEM((HALF, D), BF),
            pltpu.VMEM((HALF, D), BF),
            pltpu.VMEM((HALF, D), BF),
            pltpu.VMEM((HALF, D), BF),
            pltpu.VMEM((HALF, D), BF),
            pltpu.VMEM((TOK, D), BF),
            pltpu.VMEM((TOK, D), BF),
            pltpu.VMEM((4 * ROWS, D), BF),
            pltpu.VMEM((4 * ROWS, D), BF),
            pltpu.VMEM((4 * ROWS, D), BF),
            pltpu.VMEM((4 * ROWS, D), BF),
            pltpu.VMEM((D, H), BF),
            pltpu.VMEM((D, H), BF),
            pltpu.VMEM((H, D), BF),
            pltpu.VMEM((6, ROWS), jnp.int32),
            pltpu.VMEM((6, ROWS), BF),
            pltpu.SMEM((8, 8), jnp.int32),
            pltpu.SMEM((8,), jnp.int32),
            pltpu.VMEM((ROWS, ROWS), F32),
            dma((3,)),
            dma((6,)),
            dma((n_gather, 2, HOPS + 1)),
            dma((n_gather, 2, HOPS + 1)),
            dma((n_gather, 2, 2)),
            dma((n_gather, 2, 2)),
            dma((n_gather, NX)),
            dma((n_gather, NX)),
            dma((n_gather, NX)),
            dma((n_gather, NX)),
            dma((n_back,)),
            dma((n_back,)),
            dma((n_back, NX)),
            dma((n_back, NX)),
            dma((n_back, 2, 2)),
            dma((n_back, 2, 2)),
            dma((n_back, 2, 2)),
            dma((n_back, 2, 2)),
            dma((3,)),
        ],
        compiler_params=pltpu.CompilerParams(
            collective_id=0, has_side_effects=True, vmem_limit_bytes=56 * 1024 * 1024
        ),
    )(tokens, grad_out, routes.T, gates.T, pull_list, counts, w_gate, w_up, w_down)
    return pl.pallas_call(
        copy_kernel,
        out_shape=tuple(jax.ShapeDtypeStruct(r.shape, r.dtype) for r in results),
        in_specs=[hbm] * 5,
        out_specs=(hbm,) * 5,
        scratch_shapes=[dma((5, 4))],
        compiler_params=pltpu.CompilerParams(vmem_limit_bytes=8 * 1024 * 1024),
    )(*results)


def solution(mesh):
    both = ("group", "dev")
    in_specs = (
        P(both, None), P(both, None), P(both, None), P(both, None), P(), P(),
        P(both, None, None), P(both, None, None), P(both, None, None),
    )
    out_specs = (
        P(both, None), P(both, None),
        P(both, None, None), P(both, None, None), P(both, None, None),
    )
    return jax.shard_map(shards, mesh=mesh, in_specs=in_specs, out_specs=out_specs, check_vma=False)
```

```python
import jax
import jax.numpy as jnp
from jax import lax
from jax.experimental import pallas as pl
from jax.experimental.pallas import tpu as pltpu
from jax.sharding import PartitionSpec as P

BF = jnp.bfloat16
F32 = jnp.float32
D = 2560
H = 384
ROWS = 16
CAP = 6
NX, NY, NZ = 4, 4, 8
META = 128
GATE_LANE = 64
BLK = NZ * CAP
HALF = NX * BLK
ALL = 2 * HALF
TOK = NZ * ROWS
HOPS = 4
X_CUT, DY_CUT = (1280, 1280), (1280, 1280)
OUT_CUT, DX_CUT = (1280, 1280), (1280, 1280)
ORDER = (0, 1, 7, 2, 6, 3, 5, 4)
EARLY = 16
MESH = pl.DeviceIdType.MESH


def cut(widths):
    starts = [sum(widths[:n]) for n in range(len(widths))]
    return list(zip(starts, widths))


def nn(a, b):
    return lax.dot_general(a, b, (((1,), (0,)), ((), ())), preferred_element_type=F32)


def nt(a, b):
    return lax.dot_general(a, b, (((1,), (1,)), ((), ())), preferred_element_type=F32)


def tn(a, b):
    return lax.dot_general(a, b, (((0,), (0,)), ((), ())), preferred_element_type=F32)


def rows(i, n):
    return pl.ds(pl.multiple_of(i * n, n), n)


def kernel(
    tokens, grad_out, routes_hbm, gates_hbm, pull_hbm, counts_hbm, wg_hbm, wu_hbm, wd_hbm,
    mixed, token_grad, gg_hbm, gu_hbm, gd_hbm,
    bm, bx, bdy, sx, sdy, rx, rdy, wg, wu, wd, sel, sel_gate,
    act, slope, hid, gpre, part, far_out, far_dx, near_out, near_dx,
    back_out, back_dx, got_out, got_dx, pout, pdx, via_out, via_dx, end_out, end_dx, gg, gu, gd,
    routes, gates, pull_list, counts, chosen_t, w_sem, t_sem, z_send, z_recv, y_send, y_recv,
    x_send, x_recv, c_send, c_recv, e_send, e_recv, b_send, b_recv, a_send, a_recv, p_send, p_recv, g_sem,
):
    g = lax.axis_index("group")
    d = lax.axis_index("dev")
    y, z_lo = g // 2, g % 2
    z_hi, x, c = d // 8, (d // 2) % 4, d % 2
    z = z_hi * 2 + z_lo

    def device(x_, y_, z_, c_):
        return (y_ * 2 + z_ % 2, ((z_ // 2) * NX + x_) * 2 + c_)

    y_prev = jnp.where(z_lo == 1, y, (y + NY - 1) % NY)
    y_next = jnp.where(z_lo == 0, y, (y + 1) % NY)

    def z_taker(k):
        return device(x, y if k % 2 == 0 else y_prev, (z + k) % NZ, c)

    def z_owner(k):
        return device(x, y if k % 2 == 0 else y_next, (z + k) % NZ, c)

    sibling = device(x, y, z, 1 - c)
    y_back = device(x, (y + NY - 1) % NY, z, c)

    barrier = pltpu.get_barrier_semaphore()
    near = [z_taker(1), z_taker(7), z_owner(1), z_owner(7), z_taker(2), z_taker(6)]
    near += [y_back, device(x, (y + 1) % NY, z, c), sibling]
    near += [device((x + k) % NX, y, z, c) for k in range(1, NX)]
    for other in near:
        pl.semaphore_signal(barrier, inc=1, device_id=other, device_id_type=MESH)
    mine = rows(z, ROWS)
    r_copies = [
        pltpu.make_async_copy(src, dst, t_sem.at[2 + i])
        for i, (src, dst) in enumerate(
            ((routes_hbm, routes), (gates_hbm, gates), (pull_hbm, pull_list), (counts_hbm, counts))
        )
    ]
    t_copies = [
        pltpu.make_async_copy(tokens, bx.at[mine], t_sem.at[0]),
        pltpu.make_async_copy(grad_out, bdy.at[mine], t_sem.at[1]),
    ]
    w_copies = [
        pltpu.make_async_copy(src.at[0], dst, w_sem.at[i])
        for i, (src, dst) in enumerate(((wg_hbm, wg), (wu_hbm, wu), (wd_hbm, wd)))
    ]
    for copy in r_copies + t_copies:
        copy.start()
    for copy in r_copies:
        copy.wait()

    route = routes[...]
    expert = g * 16 + route
    for j in range(8):
        expert = jnp.where(route == 16 + j, pull_list[g, j], expert)
    token = d * ROWS + lax.broadcasted_iota(jnp.int32, route.shape, 1)
    expert = jnp.where(token < counts[g], expert, -1)
    chosen_t[...] = jnp.zeros_like(chosen_t)
    chosen_t[:6, :] = expert.astype(F32)
    chosen_t[8:14, :] = gates[...].astype(F32)
    k_row = lax.broadcasted_iota(jnp.int32, (ROWS, META), 0)
    k_lane = lax.broadcasted_iota(jnp.int32, (ROWS, META), 1)
    spread = (k_lane == k_row) & (k_row < 8) | (k_lane == k_row + (GATE_LANE - 8)) & (k_row >= 8)
    meta_in = tn(chosen_t[...].astype(BF), jnp.where(spread, 1.0, 0.0).astype(BF))
    bm[mine, :] = meta_in.astype(BF)
    for copy in t_copies:
        copy.wait()
    pl.semaphore_wait(barrier, len(near))

    sent = []

    def send(src, dst, s_sem, r_sem, to):
        copy = pltpu.make_async_remote_copy(
            src_ref=src, dst_ref=dst, send_sem=s_sem, recv_sem=r_sem,
            device_id=to, device_id_type=MESH,
        )
        copy.start()
        sent.append(copy)

    def arrived(dst, s_sem, r_sem):
        pltpu.make_async_remote_copy(
            src_ref=dst, dst_ref=dst, send_sem=s_sem, recv_sem=r_sem,
            device_id=sibling, device_id_type=MESH,
        ).wait_recv()

    pieces = [(bm, 0, META)]
    pieces += [(bx, lo, width) for lo, width in cut(X_CUT)] + [(bdy, lo, width) for lo, width in cut(DY_CUT)]
    x_pieces = list(range(1, 1 + len(X_CUT)))
    dy_pieces = list(range(1 + len(X_CUT), len(pieces)))
    ring = (device(x, y, (z + 1) % NZ, c), device(x, y, (z + NZ - 1) % NZ, c))
    skip = (device(x, y, (z + 2) % NZ, c), device(x, y, (z + NZ - 2) % NZ, c))

    def slot(block, odd):
        return rows(jnp.where((odd == 1) & (block % 2 == 0), NZ + block // 2, block), ROWS)

    def ring_block(way, step):
        return (z + NZ - step) % NZ if way == 0 else (z + step) % NZ

    def by_core(first, second):
        return jnp.where(c == 0, first, second)

    def pass_on(i, way, block, step):
        buf, lo, width = pieces[i]
        at = pl.ds(lo, width)
        send(
            buf.at[slot(block, z_lo), at], buf.at[slot(block, 1 - z_lo), at],
            z_send.at[i, way, step], z_recv.at[i, way, step], ring[way],
        )

    def pass_last(i):
        buf, lo, width = pieces[i]
        at = pl.ds(lo, width)
        block = by_core(ring_block(0, 3), ring_block(1, 3))
        there = by_core((z + 1) % NZ, (z + NZ - 1) % NZ)
        send(
            buf.at[slot(block, z_lo), at], buf.at[slot(block, 1 - z_lo), at],
            z_send.at[i, 0, HOPS], z_recv.at[i, 0, HOPS], device(x, y, there, c),
        )

    def ring_arrived(i, way, step):
        buf, lo, width = pieces[i]
        arrived(buf.at[slot(ring_block(way, step), z_lo), pl.ds(lo, width)], z_send.at[i, way, 0], z_recv.at[i, way, step])

    def y_copy(i, way, step):
        buf, lo, width = pieces[i]
        block, at = ring_block(way, step), pl.ds(lo, width)
        return pltpu.make_async_remote_copy(
            src_ref=buf.at[slot(block, z_lo), at], dst_ref=buf.at[rows(block, ROWS), at],
            send_sem=y_send.at[i, way, step // 2], recv_sem=y_recv.at[i, way, step // 2],
            device_id=y_back, device_id_type=MESH,
        )

    def y_arrived(i, step):
        @pl.when(z_lo == 1)
        def _():
            for way in range(2):
                y_copy(i, way, step).wait_recv()

    def start(i):
        for way in range(2):
            pass_on(i, way, z, 1)

    def relay(i, step):
        for way in range(2):
            ring_arrived(i, way, step)
            if step < 3:
                pass_on(i, way, ring_block(way, step), step + 1)
            if step != 2:
                pl.when(z_lo == 1)(lambda: y_copy(i, way, step).start())
        if step == 3:
            pass_last(i)

    def gathered(i):
        ring_arrived(i, 0, HOPS)
        y_arrived(i, 3)

    def ordered(buf, lo, hi, at):
        return jnp.concatenate([buf[rows((z + ORDER[n]) % NZ, ROWS), at] for n in range(lo, hi)], axis=0)

    def choices(lo, hi):
        meta = ordered(bm, lo, hi, slice(None)).astype(F32)
        n = meta.shape[0]
        lane = lax.broadcasted_iota(jnp.int32, (n, META), 1)
        gate_at = pltpu.roll(meta, GATE_LANE, 1)
        first = (g * 16 + z_hi * NX).astype(F32)
        hits, gate_of = [], []
        hit_all = jnp.zeros((n, META), F32)
        for j in range(NX):
            match = jnp.where((meta == first + j) & (lane < 6), 1.0, 0.0)
            hits.append(jnp.sum(match, axis=1, keepdims=True))
            gate_of.append(jnp.sum(match * gate_at, axis=1, keepdims=True))
            hit_all = hit_all + jnp.where(lane == j, hits[j], 0.0)
        t_row = lax.broadcasted_iota(jnp.int32, (n, n), 0)
        t_col = lax.broadcasted_iota(jnp.int32, (n, n), 1)
        before = jnp.where((t_col < t_row) & (t_col // ROWS == t_row // ROWS), 1.0, 0.0)
        rank_all = nn(before.astype(BF), hit_all.astype(BF))
        ranks = [jnp.sum(jnp.where(lane == j, rank_all, 0.0), axis=1, keepdims=True) for j in range(NX)]
        return hits, gate_of, ranks

    def selectors(chosen, lo, first, count):
        hits, gate_of, ranks = chosen
        n = hits[0].shape[0]
        q = lax.broadcasted_iota(jnp.int32, (n, NX * count), 1)
        block = lax.broadcasted_iota(jnp.int32, (n, NX * count), 0) // ROWS + lo
        place = jnp.zeros((n, NX * count), F32)
        hit_q = jnp.zeros((n, NX * count), F32)
        gate_q = jnp.zeros((n, NX * count), F32)
        start_q = jnp.zeros((n, NX * count), jnp.int32)
        for j in range(NX):
            inside = (q >= j * count) & (q < (j + 1) * count)
            start_q = jnp.where(inside, j * count, start_q)
            place = jnp.where(inside, ranks[j], place)
            hit_q = jnp.where(inside, hits[j], hit_q)
            gate_q = jnp.where(inside, gate_of[j], gate_q)
        placed = place + (block * CAP).astype(F32) == (q - start_q + first).astype(F32)
        picked = jnp.where(placed, hit_q, 0.0)
        return picked.astype(BF), (picked * gate_q).astype(BF)

    my_slot = rows(c * NX + x, BLK)
    dests = {i: (sx, rx) for i in x_pieces} | {i: (sdy, rdy) for i in dy_pieces}
    first_of = {x_pieces[0]: 0, dy_pieces[0]: len(pieces)}

    def hand_out(out, got, at, lo, count, n):
        here = pl.ds(pl.multiple_of((c * NX + x) * BLK + lo, 16), count)
        for k in (2, 1, 3):
            j = (x + k) % NX
            there = pl.ds(pl.multiple_of(j * BLK + lo, 16), count)
            send(out.at[there, at], got.at[here, at], x_send.at[n, k], x_recv.at[n, x], device(j, y, z, c))
        got[here, at] = out[pl.ds(pl.multiple_of(x * BLK + lo, 16), count), at]

    def dispatch_early(todo, selector):
        for i in todo:
            y_arrived(i, 1)
        buf, (out, got) = pieces[todo[0]][0], dests[todo[0]]
        picked = tn(selector, ordered(buf, 0, 3, slice(None))).astype(BF)
        for j in range(NX):
            out[j * BLK:j * BLK + EARLY, :] = picked[j * EARLY:(j + 1) * EARLY, :]
        hand_out(out, got, pl.ds(0, D), 0, EARLY, first_of[todo[0]])

    def dispatch(i, selector):
        buf, lo, width = pieces[i]
        out, got = dests[i]
        at = pl.ds(lo, width)
        gathered(i)
        picked = tn(selector, ordered(buf, 2, NZ, at)).astype(BF)
        late = BLK - EARLY
        for j in range(NX):
            out[j * BLK + EARLY:(j + 1) * BLK, at] = picked[j * late:(j + 1) * late, :]
        hand_out(out, got, at, EARLY, late, i)
        send(got.at[my_slot, at], got.at[my_slot, at], c_send.at[i, 0], c_recv.at[i, x], sibling)

    def share(i):
        at, got = pl.ds(*pieces[i][1:]), dests[i][1]
        for k in (1, 3, 2):
            j = (x + k) % NX
            here = got.at[rows(c * NX + j, BLK), at]
            if i in first_of:
                n, early_rows = first_of[i], pl.ds(pl.multiple_of((c * NX + j) * BLK, 16), EARLY)
                arrived(got.at[early_rows], x_send.at[n, 0], x_recv.at[n, j])
            late_rows = pl.ds(pl.multiple_of((c * NX + j) * BLK + EARLY, 16), BLK - EARLY)
            arrived(got.at[late_rows, at], x_send.at[i, 0], x_recv.at[i, j])
            send(here, here, c_send.at[i, k], c_recv.at[i, j], sibling)

    def shared(i):
        at, got = pl.ds(*pieces[i][1:]), dests[i][1]
        for k in range(NX):
            j = (x + k) % NX
            arrived(got.at[rows((1 - c) * NX + j, BLK), at], c_send.at[i, 0], c_recv.at[i, j])

    start(0)
    for i in x_pieces:
        start(i)
    for copy in w_copies:
        copy.start()
    for i in [0] + x_pieces:
        relay(i, 1)
    for i in [0] + x_pieces:
        relay(i, 2)
    for i in dy_pieces:
        start(i)
    y_arrived(0, 1)
    early_sel, early_gate = selectors(choices(0, 3), 0, 0, EARLY)
    dispatch_early(x_pieces, early_sel)
    for i in [0] + x_pieces:
        relay(i, 3)
    for i in dy_pieces:
        relay(i, 1)
    gathered(0)
    chosen = choices(0, NZ)
    late_sel, late_gate = selectors([[v[2 * ROWS:] for v in vs] for vs in chosen], 2, EARLY, BLK - EARLY)
    dispatch(x_pieces[0], late_sel)
    for i in dy_pieces:
        relay(i, 2)
    for i in x_pieces[1:]:
        dispatch(i, late_sel)
    dispatch_early(dy_pieces, early_gate)
    for i in dy_pieces:
        relay(i, 3)
    for i in dy_pieces:
        dispatch(i, late_gate)
    sel[...], sel_gate[...] = selectors(chosen, 0, 0, BLK)

    for copy in w_copies:
        copy.wait()
    pre_gate, pre_up = act, slope
    for n, i in enumerate(x_pieces):
        share(i)
        shared(i)
        at = pl.ds(*pieces[i][1:])
        by_gate, by_up = nn(rx[:, at], wg[at, :]), nn(rx[:, at], wu[at, :])
        pre_gate[...] = by_gate if n == 0 else pre_gate[...] + by_gate
        pre_up[...] = by_up if n == 0 else pre_up[...] + by_up
    v_gate, v_up = pre_gate[...], pre_up[...]
    sig = jax.nn.sigmoid(v_gate)
    silu = v_gate * sig
    hid[...] = (silu * v_up).astype(BF)
    act[...] = silu
    slope[...] = v_up * sig * (1.0 + v_gate * (1.0 - sig))

    far_rows, own_rows = rows(1 - c, HALF), rows(c, HALF)
    back_pieces = [(0, lo, width) for lo, width in cut(OUT_CUT)] + [(1, lo, width) for lo, width in cut(DX_CUT)]
    out_back, dx_back = list(range(len(OUT_CUT))), list(range(len(OUT_CUT), len(back_pieces)))
    buffers = (
        (far_out, near_out, back_out, got_out, pout, via_out, end_out),
        (far_dx, near_dx, back_dx, got_dx, pdx, via_dx, end_dx),
    )

    def rows_of(s, r, at):
        if s == 0:
            return nn(hid[r, :], wd[:, at])
        return nt(gpre[r, :H], wg[at, :]) + nt(gpre[r, H:], wu[at, :])

    def back(todo):
        for i in todo:
            s, lo, width = back_pieces[i]
            far, near_in = buffers[s][:2]
            at = pl.ds(lo, width)
            far[:, at] = rows_of(s, far_rows, at).astype(BF)
            send(far.at[:, at], near_in.at[:, at], e_send.at[i], e_recv.at[i], sibling)
        for i in todo:
            s, lo, width = back_pieces[i]
            at = pl.ds(lo, width)
            part[:, at] = rows_of(s, own_rows, at)

    def give_back(i):
        s, lo, width = back_pieces[i]
        _, near_in, summed, got = buffers[s][:4]
        at = pl.ds(lo, width)
        arrived(near_in.at[:, at], e_send.at[i], e_recv.at[i])
        summed[:, at] = (part[:, at] + near_in[:, at].astype(F32)).astype(BF)
        for k in (2, 1, 3):
            j = (x + k) % NX
            send(
                summed.at[rows(j, BLK), at], got.at[rows(x, BLK), at],
                b_send.at[i, k], b_recv.at[i, x], device(j, y, z, c),
            )
        got[rows(x, BLK), at] = summed[rows(x, BLK), at]

    def combine(i, selector):
        s, lo, width = back_pieces[i]
        got, partial, via, end = buffers[s][3:]
        at = pl.ds(lo, width)
        for k in range(1, NX):
            j = (x + k) % NX
            arrived(got.at[rows(j, BLK), at], b_send.at[i, 0], b_recv.at[i, j])
        partial[:, at] = nn(selector[...], got[:, at]).astype(BF)
        for n, (block, to) in enumerate((
            (5, skip[0]),
            (6, skip[1]),
            (7, device(x, y, by_core((z + 2) % NZ, (z + 6) % NZ), c)),
        )):
            send(partial.at[rows(block, ROWS), at], via.at[rows(n, ROWS), at], a_send.at[i, n], a_recv.at[i, n], to)
        plain = by_core((z + 6) % NZ, (z + 2) % NZ)
        send(partial.at[rows(by_core(4, 3), ROWS), at], end.at[rows(3, ROWS), at], p_send.at[i, 3], p_recv.at[i, 3], device(x, y, plain, c))

    def send_home(i):
        s, lo, width = back_pieces[i]
        partial, via, end = buffers[s][4:]
        at = pl.ds(lo, width)
        inner = by_core((z + 2) % NZ, (z + 6) % NZ)
        for n, (block, to) in enumerate((
            (1, z_owner(1)), (2, z_owner(7)), (by_core(3, 4), device(x, y, inner, c)),
        )):
            here, spot = rows(n, ROWS), rows(block, ROWS)
            arrived(via.at[here, at], a_send.at[i, n], a_recv.at[i, n])
            partial[spot, at] = (partial[spot, at].astype(F32) + via[here, at].astype(F32)).astype(BF)
            send(partial.at[spot, at], end.at[here, at], p_send.at[i, n], p_recv.at[i, n], to)

    def finish(i, result):
        s, lo, width = back_pieces[i]
        partial, _, end = buffers[s][4:]
        at = pl.ds(lo, width)
        total = partial[:ROWS, at].astype(F32)
        for n in (3, 0, 1, 2):
            here = rows(n, ROWS)
            arrived(end.at[here, at], p_send.at[i, n], p_recv.at[i, n])
            total = total + end[here, at].astype(F32)
        result[:, at] = total.astype(BF)

    back(out_back)
    for i in out_back:
        give_back(i)
    back_hidden = jnp.zeros((ALL, H), F32)
    for i in dy_pieces:
        share(i)
        shared(i)
        at = pl.ds(*pieces[i][1:])
        back_hidden = back_hidden + nt(rdy[:, at], wd[:, at])
    gpre[:, :H] = (back_hidden * slope[...]).astype(BF)
    gpre[:, H:] = (back_hidden * act[...]).astype(BF)
    back(dx_back)
    early = len(sent)
    for i in dx_back:
        give_back(i)
    combine(out_back[0], sel_gate)

    for lo in range(0, D, 1280):
        at = pl.ds(lo, 1280)
        both = tn(rx[:, at], gpre[...])
        gg[at, :] = both[:, :H].astype(BF)
        gu[at, :] = both[:, H:].astype(BF)
        gd[:, at] = tn(hid[...], rdy[:, at]).astype(BF)
    g_copies = [
        pltpu.make_async_copy(src, dst.at[0], g_sem.at[i])
        for i, (src, dst) in enumerate(((gg, gg_hbm), (gu, gu_hbm), (gd, gd_hbm)))
    ]
    for copy in g_copies:
        copy.start()
    for copy in sent[:early]:
        copy.wait_send()

    todo = [(i, sel_gate) for i in out_back[1:]] + [(i, sel) for i in dx_back]
    last = out_back[0]
    for i, selector in todo:
        combine(i, selector)
        send_home(last)
        last = i
    send_home(last)
    for i in out_back:
        finish(i, mixed)
    for i in dx_back:
        finish(i, token_grad)
    for copy in sent[early:]:
        copy.wait_send()

    @pl.when(z_lo == 1)
    def _():
        for i in range(len(pieces)):
            for way in range(2):
                for step in (1, 3):
                    y_copy(i, way, step).wait_send()

    for copy in g_copies:
        copy.wait()


def copy_kernel(*refs):
    n = (len(refs) - 1) // 2
    sems = refs[-1]
    copies = []
    for i in range(n):
        src, dst = refs[i], refs[n + i]
        if len(src.shape) == 2:
            copies.append(pltpu.make_async_copy(src, dst, sems.at[i, 0]))
            continue
        part = src.shape[1] // 4
        for j in range(4):
            at = pl.ds(j * part, part)
            copies.append(pltpu.make_async_copy(src.at[0, at], dst.at[0, at], sems.at[i, j]))
    for copy in copies:
        copy.start()
    for copy in copies:
        copy.wait()


def shards(tokens, grad_out, routes, gates, pull_list, counts, w_gate, w_up, w_down):
    vmem = pl.BlockSpec(memory_space=pltpu.VMEM)
    hbm = pl.BlockSpec(memory_space=pl.ANY)
    dma = pltpu.SemaphoreType.DMA
    n_gather = 1 + len(X_CUT) + len(DY_CUT)
    n_back = len(OUT_CUT) + len(DX_CUT)
    results = pl.pallas_call(
        kernel,
        out_shape=(
            pltpu.VMEM((ROWS, D), BF),
            pltpu.VMEM((ROWS, D), BF),
            pltpu.VMEM((1, D, H), BF),
            pltpu.VMEM((1, D, H), BF),
            pltpu.VMEM((1, H, D), BF),
        ),
        in_specs=[pl.BlockSpec(memory_space=pltpu.HBM)] * 9,
        out_specs=(vmem, vmem, hbm, hbm, hbm),
        scratch_shapes=[
            pltpu.VMEM((TOK + TOK // 2, META), BF),
            pltpu.VMEM((TOK + TOK // 2, D), BF),
            pltpu.VMEM((TOK + TOK // 2, D), BF),
            pltpu.VMEM((HALF, D), BF),
            pltpu.VMEM((HALF, D), BF),
            pltpu.VMEM((ALL, D), BF),
            pltpu.VMEM((ALL, D), BF),
            pltpu.VMEM((D, H), BF),
            pltpu.VMEM((D, H), BF),
            pltpu.VMEM((H, D), BF),
            pltpu.VMEM((TOK, HALF), BF),
            pltpu.VMEM((TOK, HALF), BF),
            pltpu.VMEM((ALL, H), F32),
            pltpu.VMEM((ALL, H), F32),
            pltpu.VMEM((ALL, H), BF),
            pltpu.VMEM((ALL, 2 * H), BF),
            pltpu.VMEM((HALF, D), F32),
            pltpu.VMEM((HALF, D), BF),
            pltpu.VMEM((HALF, D), BF),
            pltpu.VMEM((HALF, D), BF),
            pltpu.VMEM((HALF, D), BF),
            pltpu.VMEM((HALF, D), BF),
            pltpu.VMEM((HALF, D), BF),
            pltpu.VMEM((HALF, D), BF),
            pltpu.VMEM((HALF, D), BF),
            pltpu.VMEM((TOK, D), BF),
            pltpu.VMEM((TOK, D), BF),
            pltpu.VMEM((4 * ROWS, D), BF),
            pltpu.VMEM((4 * ROWS, D), BF),
            pltpu.VMEM((4 * ROWS, D), BF),
            pltpu.VMEM((4 * ROWS, D), BF),
            pltpu.VMEM((D, H), BF),
            pltpu.VMEM((D, H), BF),
            pltpu.VMEM((H, D), BF),
            pltpu.VMEM((6, ROWS), jnp.int32),
            pltpu.VMEM((6, ROWS), BF),
            pltpu.SMEM((8, 8), jnp.int32),
            pltpu.SMEM((8,), jnp.int32),
            pltpu.VMEM((ROWS, ROWS), F32),
            dma((3,)),
            dma((6,)),
            dma((n_gather, 2, HOPS + 1)),
            dma((n_gather, 2, HOPS + 1)),
            dma((n_gather, 2, 2)),
            dma((n_gather, 2, 2)),
            dma((n_gather + 1, NX)),
            dma((n_gather + 1, NX)),
            dma((n_gather, NX)),
            dma((n_gather, NX)),
            dma((n_back,)),
            dma((n_back,)),
            dma((n_back, NX)),
            dma((n_back, NX)),
            dma((n_back, 3)),
            dma((n_back, 3)),
            dma((n_back, 4)),
            dma((n_back, 4)),
            dma((3,)),
        ],
        compiler_params=pltpu.CompilerParams(
            collective_id=0, has_side_effects=True, vmem_limit_bytes=56 * 1024 * 1024
        ),
    )(tokens, grad_out, routes.T, gates.T, pull_list, counts, w_gate, w_up, w_down)
    return pl.pallas_call(
        copy_kernel,
        out_shape=tuple(jax.ShapeDtypeStruct(r.shape, r.dtype) for r in results),
        in_specs=[hbm] * 5,
        out_specs=(hbm,) * 5,
        scratch_shapes=[dma((5, 4))],
        compiler_params=pltpu.CompilerParams(vmem_limit_bytes=8 * 1024 * 1024),
    )(*results)


def solution(mesh):
    both = ("group", "dev")
    in_specs = (
        P(both, None), P(both, None), P(both, None), P(both, None), P(), P(),
        P(both, None, None), P(both, None, None), P(both, None, None),
    )
    out_specs = (
        P(both, None), P(both, None),
        P(both, None, None), P(both, None, None), P(both, None, None),
    )
    return jax.shard_map(shards, mesh=mesh, in_specs=in_specs, out_specs=out_specs, check_vma=False)
```

```python
import jax
import jax.numpy as jnp
from jax import lax
from jax.experimental import pallas as pl
from jax.experimental.pallas import tpu as pltpu
from jax.sharding import PartitionSpec as P

BF = jnp.bfloat16
F32 = jnp.float32
D = 2560
H = 384
ROWS = 16
CAP = 6
NX, NY, NZ = 4, 4, 8
META = 128
GATE_LANE = 64
BLK = NZ * CAP
HALF = NX * BLK
ALL = 2 * HALF
TOK = NZ * ROWS
HOPS = 4
X_CUT, DY_CUT = (1280, 1280), (1280, 1280)
OUT_CUT, DX_CUT = (1280, 1280), (1280, 1280)
ORDER = (0, 1, 7, 2, 6, 3, 5, 4)
EARLY = 16
MESH = pl.DeviceIdType.MESH


def cut(widths):
    starts = [sum(widths[:n]) for n in range(len(widths))]
    return list(zip(starts, widths))


def nn(a, b):
    return lax.dot_general(a, b, (((1,), (0,)), ((), ())), preferred_element_type=F32)


def nt(a, b):
    return lax.dot_general(a, b, (((1,), (1,)), ((), ())), preferred_element_type=F32)


def tn(a, b):
    return lax.dot_general(a, b, (((0,), (0,)), ((), ())), preferred_element_type=F32)


def rows(i, n):
    return pl.ds(pl.multiple_of(i * n, n), n)


def kernel(
    tokens, grad_out, routes_hbm, gates_hbm, pull_hbm, counts_hbm, wg_hbm, wu_hbm, wd_hbm,
    mixed, token_grad, gg_hbm, gu_hbm, gd_hbm,
    bm, bx, bdy, sx, sdy, rx, rdy, wg, wu, wd, sel, sel_gate,
    act, slope, hid, gpre, part, far_out, far_dx, near_out, near_dx,
    back_out, back_dx, got_out, got_dx, pout, pdx, via_out, via_dx, end_out, end_dx, gg, gu, gd,
    routes, gates, pull_list, counts, chosen_t, w_sem, t_sem, z_send, z_recv, y_send, y_recv,
    x_send, x_recv, c_send, c_recv, e_send, e_recv, b_send, b_recv, a_send, a_recv, p_send, p_recv, g_sem,
):
    g = lax.axis_index("group")
    d = lax.axis_index("dev")
    y, z_lo = g // 2, g % 2
    z_hi, x, c = d // 8, (d // 2) % 4, d % 2
    z = z_hi * 2 + z_lo

    def device(x_, y_, z_, c_):
        return (y_ * 2 + z_ % 2, ((z_ // 2) * NX + x_) * 2 + c_)

    y_prev = jnp.where(z_lo == 1, y, (y + NY - 1) % NY)
    y_next = jnp.where(z_lo == 0, y, (y + 1) % NY)

    def z_taker(k):
        return device(x, y if k % 2 == 0 else y_prev, (z + k) % NZ, c)

    def z_owner(k):
        return device(x, y if k % 2 == 0 else y_next, (z + k) % NZ, c)

    sibling = device(x, y, z, 1 - c)
    y_back = device(x, (y + NY - 1) % NY, z, c)

    barrier = pltpu.get_barrier_semaphore()
    near = [z_taker(1), z_taker(7), z_owner(1), z_owner(7), z_taker(2), z_taker(6)]
    near += [y_back, device(x, (y + 1) % NY, z, c), sibling]
    near += [device((x + k) % NX, y, z, c) for k in range(1, NX)]
    for other in near:
        pl.semaphore_signal(barrier, inc=1, device_id=other, device_id_type=MESH)
    mine = rows(z, ROWS)
    r_copies = [
        pltpu.make_async_copy(src, dst, t_sem.at[2 + i])
        for i, (src, dst) in enumerate(
            ((routes_hbm, routes), (gates_hbm, gates), (pull_hbm, pull_list), (counts_hbm, counts))
        )
    ]
    t_copies = [
        pltpu.make_async_copy(tokens, bx.at[mine], t_sem.at[0]),
        pltpu.make_async_copy(grad_out, bdy.at[mine], t_sem.at[1]),
    ]
    w_copies = [
        pltpu.make_async_copy(src.at[0], dst, w_sem.at[i])
        for i, (src, dst) in enumerate(((wg_hbm, wg), (wu_hbm, wu), (wd_hbm, wd)))
    ]
    for copy in r_copies + t_copies:
        copy.start()
    for copy in r_copies:
        copy.wait()

    route = routes[...]
    expert = g * 16 + route
    for j in range(8):
        expert = jnp.where(route == 16 + j, pull_list[g, j], expert)
    token = d * ROWS + lax.broadcasted_iota(jnp.int32, route.shape, 1)
    expert = jnp.where(token < counts[g], expert, -1)
    chosen_t[...] = jnp.zeros_like(chosen_t)
    chosen_t[:6, :] = expert.astype(F32)
    chosen_t[8:14, :] = gates[...].astype(F32)
    k_row = lax.broadcasted_iota(jnp.int32, (ROWS, META), 0)
    k_lane = lax.broadcasted_iota(jnp.int32, (ROWS, META), 1)
    spread = (k_lane == k_row) & (k_row < 8) | (k_lane == k_row + (GATE_LANE - 8)) & (k_row >= 8)
    meta_in = tn(chosen_t[...].astype(BF), jnp.where(spread, 1.0, 0.0).astype(BF))
    bm[mine, :] = meta_in.astype(BF)
    for copy in t_copies:
        copy.wait()
    pl.semaphore_wait(barrier, len(near))

    sent = []

    def send(src, dst, s_sem, r_sem, to):
        copy = pltpu.make_async_remote_copy(
            src_ref=src, dst_ref=dst, send_sem=s_sem, recv_sem=r_sem,
            device_id=to, device_id_type=MESH,
        )
        copy.start()
        sent.append(copy)

    def arrived(dst, s_sem, r_sem):
        pltpu.make_async_remote_copy(
            src_ref=dst, dst_ref=dst, send_sem=s_sem, recv_sem=r_sem,
            device_id=sibling, device_id_type=MESH,
        ).wait_recv()

    pieces = [(bm, 0, META)]
    pieces += [(bx, lo, width) for lo, width in cut(X_CUT)] + [(bdy, lo, width) for lo, width in cut(DY_CUT)]
    x_pieces = list(range(1, 1 + len(X_CUT)))
    dy_pieces = list(range(1 + len(X_CUT), len(pieces)))
    ring = (device(x, y, (z + 1) % NZ, c), device(x, y, (z + NZ - 1) % NZ, c))
    skip = (device(x, y, (z + 2) % NZ, c), device(x, y, (z + NZ - 2) % NZ, c))

    def slot(block, odd):
        return rows(jnp.where((odd == 1) & (block % 2 == 0), NZ + block // 2, block), ROWS)

    def ring_block(way, step):
        return (z + NZ - step) % NZ if way == 0 else (z + step) % NZ

    def by_core(first, second):
        return jnp.where(c == 0, first, second)

    def pass_on(i, way, block, step):
        buf, lo, width = pieces[i]
        at = pl.ds(lo, width)
        send(
            buf.at[slot(block, z_lo), at], buf.at[slot(block, 1 - z_lo), at],
            z_send.at[i, way, step], z_recv.at[i, way, step], ring[way],
        )

    def pass_last(i):
        buf, lo, width = pieces[i]
        at = pl.ds(lo, width)
        block = by_core(ring_block(0, 3), ring_block(1, 3))
        there = by_core((z + 1) % NZ, (z + NZ - 1) % NZ)
        send(
            buf.at[slot(block, z_lo), at], buf.at[slot(block, 1 - z_lo), at],
            z_send.at[i, 0, HOPS], z_recv.at[i, 0, HOPS], device(x, y, there, c),
        )

    def ring_arrived(i, way, step):
        buf, lo, width = pieces[i]
        arrived(buf.at[slot(ring_block(way, step), z_lo), pl.ds(lo, width)], z_send.at[i, way, 0], z_recv.at[i, way, step])

    def y_copy(i, way, step):
        buf, lo, width = pieces[i]
        block, at = ring_block(way, step), pl.ds(lo, width)
        return pltpu.make_async_remote_copy(
            src_ref=buf.at[slot(block, z_lo), at], dst_ref=buf.at[rows(block, ROWS), at],
            send_sem=y_send.at[i, way, step // 2], recv_sem=y_recv.at[i, way, step // 2],
            device_id=y_back, device_id_type=MESH,
        )

    def y_arrived(i, step):
        @pl.when(z_lo == 1)
        def _():
            for way in range(2):
                y_copy(i, way, step).wait_recv()

    def start(i):
        for way in range(2):
            pass_on(i, way, z, 1)

    def relay(i, step):
        for way in range(2):
            ring_arrived(i, way, step)
            if step < 3:
                pass_on(i, way, ring_block(way, step), step + 1)
            if step != 2:
                pl.when(z_lo == 1)(lambda: y_copy(i, way, step).start())
        if step == 3:
            pass_last(i)

    def gathered(i):
        ring_arrived(i, 0, HOPS)
        y_arrived(i, 3)

    def ordered(buf, lo, hi, at):
        return jnp.concatenate([buf[rows((z + ORDER[n]) % NZ, ROWS), at] for n in range(lo, hi)], axis=0)

    def choices(lo, hi):
        meta = ordered(bm, lo, hi, slice(None)).astype(F32)
        n = meta.shape[0]
        lane = lax.broadcasted_iota(jnp.int32, (n, META), 1)
        gate_at = pltpu.roll(meta, GATE_LANE, 1)
        first = (g * 16 + z_hi * NX).astype(F32)
        hits, gate_of = [], []
        hit_all = jnp.zeros((n, META), F32)
        for j in range(NX):
            match = jnp.where((meta == first + j) & (lane < 6), 1.0, 0.0)
            hits.append(jnp.sum(match, axis=1, keepdims=True))
            gate_of.append(jnp.sum(match * gate_at, axis=1, keepdims=True))
            hit_all = hit_all + jnp.where(lane == j, hits[j], 0.0)
        t_row = lax.broadcasted_iota(jnp.int32, (n, n), 0)
        t_col = lax.broadcasted_iota(jnp.int32, (n, n), 1)
        before = jnp.where((t_col < t_row) & (t_col // ROWS == t_row // ROWS), 1.0, 0.0)
        rank_all = nn(before.astype(BF), hit_all.astype(BF))
        ranks = [jnp.sum(jnp.where(lane == j, rank_all, 0.0), axis=1, keepdims=True) for j in range(NX)]
        return hits, gate_of, ranks

    def selectors(chosen, lo, first, count):
        hits, gate_of, ranks = chosen
        n = hits[0].shape[0]
        q = lax.broadcasted_iota(jnp.int32, (n, NX * count), 1)
        block = lax.broadcasted_iota(jnp.int32, (n, NX * count), 0) // ROWS + lo
        place = jnp.zeros((n, NX * count), F32)
        hit_q = jnp.zeros((n, NX * count), F32)
        gate_q = jnp.zeros((n, NX * count), F32)
        start_q = jnp.zeros((n, NX * count), jnp.int32)
        for j in range(NX):
            inside = (q >= j * count) & (q < (j + 1) * count)
            start_q = jnp.where(inside, j * count, start_q)
            place = jnp.where(inside, ranks[j], place)
            hit_q = jnp.where(inside, hits[j], hit_q)
            gate_q = jnp.where(inside, gate_of[j], gate_q)
        placed = place + (block * CAP).astype(F32) == (q - start_q + first).astype(F32)
        picked = jnp.where(placed, hit_q, 0.0)
        return picked.astype(BF), (picked * gate_q).astype(BF)

    my_slot = rows(c * NX + x, BLK)
    dests = {i: (sx, rx) for i in x_pieces} | {i: (sdy, rdy) for i in dy_pieces}

    def hand_out(out, got, at, lo, count, n):
        here = pl.ds(pl.multiple_of((c * NX + x) * BLK + lo, 16), count)
        for k in (2, 1, 3):
            j = (x + k) % NX
            there = pl.ds(pl.multiple_of(j * BLK + lo, 16), count)
            send(out.at[there, at], got.at[here, at], x_send.at[n, k], x_recv.at[n, x], device(j, y, z, c))
        got[here, at] = out[pl.ds(pl.multiple_of(x * BLK + lo, 16), count), at]

    def dispatch_early(todo, selector):
        for i in todo:
            y_arrived(i, 1)
        buf, (out, got) = pieces[todo[0]][0], dests[todo[0]]
        picked = tn(selector, ordered(buf, 0, 3, slice(None))).astype(BF)
        for j in range(NX):
            out[j * BLK:j * BLK + EARLY, :] = picked[j * EARLY:(j + 1) * EARLY, :]
        hand_out(out, got, pl.ds(0, D), 0, EARLY, 0)

    def dispatch(i, selector):
        buf, lo, width = pieces[i]
        out, got = dests[i]
        at = pl.ds(lo, width)
        gathered(i)
        if i in dy_pieces:
            y_arrived(i, 1)
            out[:, at] = tn(selector, ordered(buf, 0, NZ, at)).astype(BF)
            hand_out(out, got, at, 0, BLK, i)
        else:
            picked = tn(selector, ordered(buf, 2, NZ, at)).astype(BF)
            late = BLK - EARLY
            for j in range(NX):
                out[j * BLK + EARLY:(j + 1) * BLK, at] = picked[j * late:(j + 1) * late, :]
            hand_out(out, got, at, EARLY, late, i)
        send(got.at[my_slot, at], got.at[my_slot, at], c_send.at[i, 0], c_recv.at[i, x], sibling)

    def share(i):
        at, got = pl.ds(*pieces[i][1:]), dests[i][1]
        for k in (1, 3, 2):
            j = (x + k) % NX
            here = got.at[rows(c * NX + j, BLK), at]
            if i == x_pieces[0]:
                early_rows = pl.ds(pl.multiple_of((c * NX + j) * BLK, 16), EARLY)
                arrived(got.at[early_rows], x_send.at[0, 0], x_recv.at[0, j])
            if i in x_pieces:
                late_rows = pl.ds(pl.multiple_of((c * NX + j) * BLK + EARLY, 16), BLK - EARLY)
                arrived(got.at[late_rows, at], x_send.at[i, 0], x_recv.at[i, j])
            else:
                arrived(here, x_send.at[i, 0], x_recv.at[i, j])
            send(here, here, c_send.at[i, k], c_recv.at[i, j], sibling)

    def shared(i):
        at, got = pl.ds(*pieces[i][1:]), dests[i][1]
        for k in range(NX):
            j = (x + k) % NX
            arrived(got.at[rows((1 - c) * NX + j, BLK), at], c_send.at[i, 0], c_recv.at[i, j])

    start(0)
    for i in x_pieces:
        start(i)
    for copy in w_copies:
        copy.start()
    for i in [0] + x_pieces:
        relay(i, 1)
    for i in [0] + x_pieces:
        relay(i, 2)
    for i in dy_pieces:
        start(i)
    y_arrived(0, 1)
    early_sel = selectors(choices(0, 3), 0, 0, EARLY)[0]
    dispatch_early(x_pieces, early_sel)
    for i in [0] + x_pieces:
        relay(i, 3)
    for i in dy_pieces:
        relay(i, 1)
    gathered(0)
    chosen = choices(0, NZ)
    late_sel = selectors([[v[2 * ROWS:] for v in vs] for vs in chosen], 2, EARLY, BLK - EARLY)[0]
    dispatch(x_pieces[0], late_sel)
    for i in dy_pieces:
        relay(i, 2)
    for i in x_pieces[1:]:
        dispatch(i, late_sel)
    sel[...], sel_gate[...] = selectors(chosen, 0, 0, BLK)
    for i in dy_pieces:
        relay(i, 3)
    for i in dy_pieces:
        dispatch(i, sel_gate[...])

    for copy in w_copies:
        copy.wait()
    pre_gate, pre_up = act, slope
    for n, i in enumerate(x_pieces):
        share(i)
        shared(i)
        at = pl.ds(*pieces[i][1:])
        by_gate, by_up = nn(rx[:, at], wg[at, :]), nn(rx[:, at], wu[at, :])
        pre_gate[...] = by_gate if n == 0 else pre_gate[...] + by_gate
        pre_up[...] = by_up if n == 0 else pre_up[...] + by_up
    v_gate, v_up = pre_gate[...], pre_up[...]
    sig = jax.nn.sigmoid(v_gate)
    silu = v_gate * sig
    hid[...] = (silu * v_up).astype(BF)
    act[...] = silu
    slope[...] = v_up * sig * (1.0 + v_gate * (1.0 - sig))

    far_rows, own_rows = rows(1 - c, HALF), rows(c, HALF)
    back_pieces = [(0, lo, width) for lo, width in cut(OUT_CUT)] + [(1, lo, width) for lo, width in cut(DX_CUT)]
    out_back, dx_back = list(range(len(OUT_CUT))), list(range(len(OUT_CUT), len(back_pieces)))
    buffers = (
        (far_out, near_out, back_out, got_out, pout, via_out, end_out),
        (far_dx, near_dx, back_dx, got_dx, pdx, via_dx, end_dx),
    )

    def rows_of(s, r, at):
        if s == 0:
            return nn(hid[r, :], wd[:, at])
        return nt(gpre[r, :H], wg[at, :]) + nt(gpre[r, H:], wu[at, :])

    def back(todo):
        for i in todo:
            s, lo, width = back_pieces[i]
            far, near_in = buffers[s][:2]
            at = pl.ds(lo, width)
            far[:, at] = rows_of(s, far_rows, at).astype(BF)
            send(far.at[:, at], near_in.at[:, at], e_send.at[i], e_recv.at[i], sibling)
        for i in todo:
            s, lo, width = back_pieces[i]
            at = pl.ds(lo, width)
            part[:, at] = rows_of(s, own_rows, at)

    def give_back(i):
        s, lo, width = back_pieces[i]
        _, near_in, summed, got = buffers[s][:4]
        at = pl.ds(lo, width)
        arrived(near_in.at[:, at], e_send.at[i], e_recv.at[i])
        summed[:, at] = (part[:, at] + near_in[:, at].astype(F32)).astype(BF)
        for k in (2, 1, 3):
            j = (x + k) % NX
            send(
                summed.at[rows(j, BLK), at], got.at[rows(x, BLK), at],
                b_send.at[i, k], b_recv.at[i, x], device(j, y, z, c),
            )
        got[rows(x, BLK), at] = summed[rows(x, BLK), at]

    def combine(i, selector):
        s, lo, width = back_pieces[i]
        got, partial, via, end = buffers[s][3:]
        at = pl.ds(lo, width)
        for k in range(1, NX):
            j = (x + k) % NX
            arrived(got.at[rows(j, BLK), at], b_send.at[i, 0], b_recv.at[i, j])
        partial[:, at] = nn(selector[...], got[:, at]).astype(BF)
        for n, (block, to) in enumerate((
            (5, skip[0]),
            (6, skip[1]),
            (7, device(x, y, by_core((z + 2) % NZ, (z + 6) % NZ), c)),
        )):
            send(partial.at[rows(block, ROWS), at], via.at[rows(n, ROWS), at], a_send.at[i, n], a_recv.at[i, n], to)
        plain = by_core((z + 6) % NZ, (z + 2) % NZ)
        send(partial.at[rows(by_core(4, 3), ROWS), at], end.at[rows(3, ROWS), at], p_send.at[i, 3], p_recv.at[i, 3], device(x, y, plain, c))

    def send_home(i):
        s, lo, width = back_pieces[i]
        partial, via, end = buffers[s][4:]
        at = pl.ds(lo, width)
        inner = by_core((z + 2) % NZ, (z + 6) % NZ)
        for n, (block, to) in enumerate((
            (1, z_owner(1)), (2, z_owner(7)), (by_core(3, 4), device(x, y, inner, c)),
        )):
            here, spot = rows(n, ROWS), rows(block, ROWS)
            arrived(via.at[here, at], a_send.at[i, n], a_recv.at[i, n])
            partial[spot, at] = (partial[spot, at].astype(F32) + via[here, at].astype(F32)).astype(BF)
            send(partial.at[spot, at], end.at[here, at], p_send.at[i, n], p_recv.at[i, n], to)

    def finish(i, result):
        s, lo, width = back_pieces[i]
        partial, _, end = buffers[s][4:]
        at = pl.ds(lo, width)
        total = partial[:ROWS, at].astype(F32)
        for n in (3, 0, 1, 2):
            here = rows(n, ROWS)
            arrived(end.at[here, at], p_send.at[i, n], p_recv.at[i, n])
            total = total + end[here, at].astype(F32)
        result[:, at] = total.astype(BF)

    back(out_back)
    for i in out_back:
        give_back(i)
    back_hidden = jnp.zeros((ALL, H), F32)
    for i in dy_pieces:
        share(i)
        shared(i)
        at = pl.ds(*pieces[i][1:])
        back_hidden = back_hidden + nt(rdy[:, at], wd[:, at])
    gpre[:, :H] = (back_hidden * slope[...]).astype(BF)
    gpre[:, H:] = (back_hidden * act[...]).astype(BF)
    back(dx_back)
    early = len(sent)
    for i in dx_back:
        give_back(i)
    combine(out_back[0], sel_gate)

    for lo in range(0, D, 1280):
        at = pl.ds(lo, 1280)
        both = tn(rx[:, at], gpre[...])
        gg[at, :] = both[:, :H].astype(BF)
        gu[at, :] = both[:, H:].astype(BF)
        gd[:, at] = tn(hid[...], rdy[:, at]).astype(BF)
    g_copies = [
        pltpu.make_async_copy(src, dst.at[0], g_sem.at[i])
        for i, (src, dst) in enumerate(((gg, gg_hbm), (gu, gu_hbm), (gd, gd_hbm)))
    ]
    for copy in g_copies:
        copy.start()
    for copy in sent[:early]:
        copy.wait_send()

    todo = [(i, sel_gate) for i in out_back[1:]] + [(i, sel) for i in dx_back]
    last = out_back[0]
    for i, selector in todo:
        combine(i, selector)
        send_home(last)
        last = i
    send_home(last)
    for i in out_back:
        finish(i, mixed)
    for i in dx_back:
        finish(i, token_grad)
    for copy in sent[early:]:
        copy.wait_send()

    @pl.when(z_lo == 1)
    def _():
        for i in range(len(pieces)):
            for way in range(2):
                for step in (1, 3):
                    y_copy(i, way, step).wait_send()

    for copy in g_copies:
        copy.wait()


def copy_kernel(*refs):
    n = (len(refs) - 1) // 2
    sems = refs[-1]
    copies = []
    for i in range(n):
        src, dst = refs[i], refs[n + i]
        if len(src.shape) == 2:
            copies.append(pltpu.make_async_copy(src, dst, sems.at[i, 0]))
            continue
        part = src.shape[1] // 4
        for j in range(4):
            at = pl.ds(j * part, part)
            copies.append(pltpu.make_async_copy(src.at[0, at], dst.at[0, at], sems.at[i, j]))
    for copy in copies:
        copy.start()
    for copy in copies:
        copy.wait()


def shards(tokens, grad_out, routes, gates, pull_list, counts, w_gate, w_up, w_down):
    vmem = pl.BlockSpec(memory_space=pltpu.VMEM)
    hbm = pl.BlockSpec(memory_space=pl.ANY)
    dma = pltpu.SemaphoreType.DMA
    n_gather = 1 + len(X_CUT) + len(DY_CUT)
    n_back = len(OUT_CUT) + len(DX_CUT)
    results = pl.pallas_call(
        kernel,
        out_shape=(
            pltpu.VMEM((ROWS, D), BF),
            pltpu.VMEM((ROWS, D), BF),
            pltpu.VMEM((1, D, H), BF),
            pltpu.VMEM((1, D, H), BF),
            pltpu.VMEM((1, H, D), BF),
        ),
        in_specs=[pl.BlockSpec(memory_space=pltpu.HBM)] * 9,
        out_specs=(vmem, vmem, hbm, hbm, hbm),
        scratch_shapes=[
            pltpu.VMEM((TOK + TOK // 2, META), BF),
            pltpu.VMEM((TOK + TOK // 2, D), BF),
            pltpu.VMEM((TOK + TOK // 2, D), BF),
            pltpu.VMEM((HALF, D), BF),
            pltpu.VMEM((HALF, D), BF),
            pltpu.VMEM((ALL, D), BF),
            pltpu.VMEM((ALL, D), BF),
            pltpu.VMEM((D, H), BF),
            pltpu.VMEM((D, H), BF),
            pltpu.VMEM((H, D), BF),
            pltpu.VMEM((TOK, HALF), BF),
            pltpu.VMEM((TOK, HALF), BF),
            pltpu.VMEM((ALL, H), F32),
            pltpu.VMEM((ALL, H), F32),
            pltpu.VMEM((ALL, H), BF),
            pltpu.VMEM((ALL, 2 * H), BF),
            pltpu.VMEM((HALF, D), F32),
            pltpu.VMEM((HALF, D), BF),
            pltpu.VMEM((HALF, D), BF),
            pltpu.VMEM((HALF, D), BF),
            pltpu.VMEM((HALF, D), BF),
            pltpu.VMEM((HALF, D), BF),
            pltpu.VMEM((HALF, D), BF),
            pltpu.VMEM((HALF, D), BF),
            pltpu.VMEM((HALF, D), BF),
            pltpu.VMEM((TOK, D), BF),
            pltpu.VMEM((TOK, D), BF),
            pltpu.VMEM((4 * ROWS, D), BF),
            pltpu.VMEM((4 * ROWS, D), BF),
            pltpu.VMEM((4 * ROWS, D), BF),
            pltpu.VMEM((4 * ROWS, D), BF),
            pltpu.VMEM((D, H), BF),
            pltpu.VMEM((D, H), BF),
            pltpu.VMEM((H, D), BF),
            pltpu.VMEM((6, ROWS), jnp.int32),
            pltpu.VMEM((6, ROWS), BF),
            pltpu.SMEM((8, 8), jnp.int32),
            pltpu.SMEM((8,), jnp.int32),
            pltpu.VMEM((ROWS, ROWS), F32),
            dma((3,)),
            dma((6,)),
            dma((n_gather, 2, HOPS + 1)),
            dma((n_gather, 2, HOPS + 1)),
            dma((n_gather, 2, 2)),
            dma((n_gather, 2, 2)),
            dma((n_gather, NX)),
            dma((n_gather, NX)),
            dma((n_gather, NX)),
            dma((n_gather, NX)),
            dma((n_back,)),
            dma((n_back,)),
            dma((n_back, NX)),
            dma((n_back, NX)),
            dma((n_back, 3)),
            dma((n_back, 3)),
            dma((n_back, 4)),
            dma((n_back, 4)),
            dma((3,)),
        ],
        compiler_params=pltpu.CompilerParams(
            collective_id=0, has_side_effects=True, vmem_limit_bytes=56 * 1024 * 1024
        ),
    )(tokens, grad_out, routes.T, gates.T, pull_list, counts, w_gate, w_up, w_down)
    return pl.pallas_call(
        copy_kernel,
        out_shape=tuple(jax.ShapeDtypeStruct(r.shape, r.dtype) for r in results),
        in_specs=[hbm] * 5,
        out_specs=(hbm,) * 5,
        scratch_shapes=[dma((5, 4))],
        compiler_params=pltpu.CompilerParams(vmem_limit_bytes=8 * 1024 * 1024),
    )(*results)


def solution(mesh):
    both = ("group", "dev")
    in_specs = (
        P(both, None), P(both, None), P(both, None), P(both, None), P(), P(),
        P(both, None, None), P(both, None, None), P(both, None, None),
    )
    out_specs = (
        P(both, None), P(both, None),
        P(both, None, None), P(both, None, None), P(both, None, None),
    )
    return jax.shard_map(shards, mesh=mesh, in_specs=in_specs, out_specs=out_specs, check_vma=False)
```
